32 devices in a mesh: group: 2 (over y), dp: 4 (over z), tensor: 4 (over x, core).
Axes of the slice: x: 2, y: 2, z: 4, core: 2. Of those that a mesh axis runs over, the one named last changes fastest.
Arguments:
- tokens: bfloat16 [5120, 8192], P(('group', 'dp'), 'tensor'), parts along dimension 0, may hold values from -6 to 6
- base_weight: bfloat16 [8192, 1024], P('tensor'), may hold values from -0.0625 to 0.0625
- down_basis: bfloat16 [8192, 256], P('tensor'), may hold values from -0.0625 to 0.0625
- up_basis: bfloat16 [256, 1024], P(None, 'tensor'), may hold values from -0.375 to 0.375
- core_bank: bfloat16 [2048, 256, 256], P('dp', 'tensor'), may hold values from -0.375 to 0.375
- request_adapter: int32 [32], P('group'), parts along dimension 0, may hold values from 0 to 2047, as said below
- request_length: int32 [32], P('group'), parts along dimension 0, may hold values from 1 to 320, as said below
- core_slot: int32 [4096], P('group'), parts along dimension 0, may hold values from 0 to 2047, as said below
Outputs:
- projected: bfloat16 [5120, 1024], P(('group', 'dp'), 'tensor'), parts along dimension 0
The draws below stay inside these ranges and needn't reach their ends.
There are 2 independent parts, one for each index of `group`. The reference program is written for one: setup_inputs(seed, part) draws one part's arguments, and reference() takes and returns one part's arrays. A program takes and returns all parts, laid end to end along the dimension named above; an argument that names none is the same for every part. Nothing has to cross between parts.
Inputs may be any that keep to these rules, and one draw needn't show every extreme that they name: `request_length`: requests are numbered home by home: requests k * 4 to (k + 1) * 4 - 1 lie in the rows of index k of dp and their lengths sum to 640; each index of dp has a request of length 320. `request_adapter`: the owner of an adapter is core_slot // 512. The requests of one index of dp use adapters of distinct owners, and in every draw one owner serves a request of length 320 of every index of dp. `core_slot`: A permutation.
All inputs are finite; a program needn't handle non-finite values.
Results may differ from the reference program's by a relative error of at most 0.0048.
Values may be sent and summed in bfloat16 or wider, within the bound.
No kernel may reach another device: no remote copies, remote signals or barrier semaphores. Data moves between devices by JAX's collectives and lax.ppermute only.
A program may use at most 128 MiB of HBM per device.

```python
import jax
import jax.numpy as jnp
from jax import lax

D = 8192
R = 256
NA = 2048
TOK_DEV = 640
OUT = 1024
OWNERS = 4
REQ_DEV = 4
MOST_LEN = 320
PER = 512
TOKENS = 2560


def permute_row(key_row, length):
    return jax.random.permutation(key_row, length)


def shared_plan(key):
    k_perm, k_shift, k_local, k_order, k_owner = jax.random.split(key, 5)
    slots = jax.random.permutation(k_perm, NA).astype(jnp.int32)
    inverse = jnp.argsort(slots).astype(jnp.int32)
    rest = TOK_DEV - MOST_LEN
    count = REQ_DEV - 1
    quota = rest // count
    extra = rest % count
    half = count // 2
    base_row = quota + (jnp.arange(count) < extra).astype(jnp.int32)
    shifts = jax.random.randint(k_shift, (OWNERS, half), -(quota - 1), quota).astype(jnp.int32)
    perturb = jnp.zeros((OWNERS, count), jnp.int32)
    perturb = perturb.at[:, :half].add(shifts)
    perturb = perturb.at[:, count - half:].add(-shifts[:, ::-1])
    others = base_row[None, :] + perturb
    full_lengths = jnp.concatenate([jnp.full((OWNERS, 1), MOST_LEN, jnp.int32), others], axis=1)
    top_owner = slots[NA - 1] // PER
    order_keys = jax.random.split(k_order, OWNERS)
    orders = jax.vmap(partial_perm_requests)(order_keys).astype(jnp.int32)
    owner_keys = jax.random.split(k_owner, OWNERS)
    rolls = jax.vmap(partial_perm_owners)(owner_keys).astype(jnp.int32)
    other_owners = (top_owner + 1 + rolls[:, :REQ_DEV - 1]) % OWNERS
    full_owners = jnp.concatenate([jnp.full((OWNERS, 1), top_owner, jnp.int32), other_owners], axis=1)
    local_pick = jax.random.randint(k_local, (OWNERS, REQ_DEV), 0, PER).astype(jnp.int32)
    local_pick = local_pick.at[0, 0].set(slots[NA - 1] % PER)
    full_adapters = inverse[full_owners * PER + local_pick]
    lengths = jnp.take_along_axis(full_lengths, orders, axis=1)
    adapters = jnp.take_along_axis(full_adapters, orders, axis=1)
    return (slots, lengths.reshape(-1).astype(jnp.int32), adapters.reshape(-1).astype(jnp.int32))


def partial_perm_requests(key_row):
    return permute_row(key_row, REQ_DEV)


def partial_perm_owners(key_row):
    return permute_row(key_row, OWNERS - 1)


def draw_request_adapter(key, part):
    plan = shared_plan(key)
    return plan[2]


def draw_request_length(key, part):
    plan = shared_plan(key)
    return plan[1]


def draw_core_slot(key, part):
    plan = shared_plan(key)
    return plan[0]


def level_of(stream_key, extent, shards, low, high):
    level, own = 1.0, jax.random.fold_in(stream_key, 6)
    for axis_at, parts in shards:
        steps = jnp.exp(jax.random.uniform(jax.random.fold_in(own, axis_at), (parts,), jnp.float32, low / len(shards), high / len(shards)))
        level = level * jnp.repeat(steps, extent[axis_at] // parts).reshape([-1 if axis == axis_at else 1 for axis in range(len(extent))])
    return level


def centred(own_key, dims, deviation, most, cuts=(), held_as=jnp.bfloat16):
    values = jax.random.normal(own_key, dims, jnp.float32) * deviation
    if len(cuts) > 0:
        values = level_of(own_key, dims, cuts, -0.22, 0.18) * values
    return jnp.clip(values, min=-most, max=most).astype(held_as)


def setup_inputs(seed: int = 0, part: int = 0) -> dict:
    seeds = jax.random.split(jax.random.key(seed), 9)
    part_splits = jax.random.split(jax.random.fold_in(seeds[8], part), 9)
    tokens = centred(part_splits[0], (TOKENS, D), 1.0, 6.0, ((0, 4), (1, 4)))
    base_weight = centred(seeds[1], (D, OUT), D ** -0.5, 0.0625, ((0, 4),))
    down_basis = centred(seeds[2], (D, R), D ** -0.5, 0.0625, ((0, 4),))
    up_basis = centred(seeds[3], (R, OUT), R ** -0.5, 0.375, ((1, 4),))
    core_bank = centred(seeds[4], (NA, R, R), R ** -0.5, 0.375, ((0, 4), (1, 4)))
    request_adapter = draw_request_adapter(jax.random.fold_in(jax.random.fold_in(seeds[8], part), 71), part)
    request_length = draw_request_length(jax.random.fold_in(jax.random.fold_in(seeds[8], part), 71), part)
    core_slot = draw_core_slot(jax.random.fold_in(jax.random.fold_in(seeds[8], part), 71), part)
    return {"tokens": tokens, "base_weight": base_weight, "down_basis": down_basis, "up_basis": up_basis, "core_bank": core_bank, "request_adapter": request_adapter, "request_length": request_length, "core_slot": core_slot}


def reference(tokens, base_weight, down_basis, up_basis, core_bank, request_adapter, request_length, core_slot):
    base = jnp.dot(tokens, base_weight, preferred_element_type=jnp.float32)
    hidden = jnp.dot(tokens, down_basis, preferred_element_type=jnp.float32).astype(jnp.bfloat16)
    request_ends = jnp.cumsum(request_length).astype(jnp.int32)
    positions = jnp.arange(TOKENS, dtype=jnp.int32)
    owning = jnp.sum((positions[:, None] >= request_ends[None, :]).astype(jnp.int32), axis=1).astype(jnp.int32)
    row_slot = core_slot[request_adapter[owning]].astype(jnp.int32)

    def per_block(pair):
        rows, slots = pair
        cores = jnp.take(core_bank, slots, axis=0).astype(jnp.float32)
        return jnp.einsum("tr,trc->tc", rows.astype(jnp.float32), cores, precision=lax.Precision.HIGHEST)

    core_sum = lax.map(per_block, (hidden.reshape(OWNERS, TOK_DEV, R), row_slot.reshape(OWNERS, TOK_DEV)))
    core_out = core_sum.reshape(TOKENS, R).astype(jnp.bfloat16)
    lifted = jnp.dot(core_out, up_basis, preferred_element_type=jnp.float32)
    return (base + lifted).astype(jnp.bfloat16)
```

```python
import functools

import jax
import jax.numpy as jnp
from jax import lax
from jax.experimental import pallas as pl
from jax.experimental.pallas import tpu as pltpu
from jax.sharding import PartitionSpec as P

F32 = jnp.float32
BF16 = jnp.bfloat16
CORES = 2
LANES = 128
VMEM_LIMIT = 40 * 1024 * 1024

ANY = pl.BlockSpec(memory_space=pl.ANY)
SMEM = pl.BlockSpec(memory_space=pltpu.SMEM)
VMEM = pl.BlockSpec(memory_space=pltpu.VMEM)


def params():
    return pltpu.CompilerParams(vmem_limit_bytes=VMEM_LIMIT)


def row_chunks(rows, parts):
    size = rows // parts
    return [(i * size, size) for i in range(parts)]


def hidden_kernel(
    sizes, place, adapters, lengths, slots, bank, tokens, down, *rest
):
    owners, req_dev, per_owner, width, block, parts = sizes
    picks, (send, keep, table) = rest[:owners], rest[owners : owners + 3]
    tok_buf, down_buf, tok_sem, down_sem, pick_sem = rest[owners + 3 :]
    chunks = row_chunks(tok_buf.shape[0], parts)
    down_copy = pltpu.make_async_copy(down, down_buf, down_sem)
    down_copy.start()
    tok_copies = []
    for i, (at, size) in enumerate(chunks):
        copy = pltpu.make_async_copy(
            tokens.at[pl.ds(at, size)], tok_buf.at[pl.ds(at, size)], tok_sem.at[i]
        )
        copy.start()
        tok_copies.append(copy)
    me, core = place[0], place[1] % CORES
    pick_copies = []
    for shift in range(owners):
        home = (me + shift) % owners
        index = jnp.int32(0)
        for q in range(req_dev):
            slot = slots[adapters[home * req_dev + q]]
            index = jnp.where(slot // per_owner == me, slot % per_owner, index)
        copy = pltpu.make_async_copy(bank.at[index], picks[shift], pick_sem.at[shift])
        copy.start()
        pick_copies.append(copy)
    for shift in range(owners):
        table[0, shift] = 0
        table[1, shift] = 0
    start = jnp.int32(0)
    for q in range(req_dev):
        owner = slots[adapters[me * req_dev + q]] // per_owner
        shift = (me - owner + owners) % owners
        end = start + lengths[me * req_dev + q]
        table[0, shift] = start
        table[1, shift] = end
        start = end
    down_copy.wait()
    for i, (at, size) in enumerate(chunks):
        tok_copies[i].wait()
        part = jnp.dot(
            tok_buf[at : at + size, :], down_buf[...], preferred_element_type=F32
        )
        halves = [
            jnp.concatenate(
                [part[:, (CORES * x + c) * block : (CORES * x + c + 1) * block] for x in range(width)],
                axis=1,
            )
            for c in range(CORES)
        ]
        send[at : at + size, :] = jnp.where(core == 0, halves[1], halves[0]).astype(BF16)
        keep[at : at + size, :] = jnp.where(core == 0, halves[0], halves[1])
    for copy in pick_copies:
        copy.wait()


def chip_kernel(width, block, place, keep, got, *rest):
    sends, own = rest[:-1], rest[-1]
    x = place[1] // CORES
    total = keep[...] + got[...].astype(F32)
    pieces = [total[:, i * block : (i + 1) * block] for i in range(width)]

    def piece(index):
        out = pieces[0]
        for i in range(1, width):
            out = jnp.where(index == i, pieces[i], out)
        return out

    own[...] = piece(x)
    pack = LANES // block
    rows = total.shape[0] // pack
    for shift in range(1, width):
        part = piece((x + shift) % width).astype(BF16)
        sends[shift - 1][...] = jnp.concatenate(
            [part[i * rows : (i + 1) * rows] for i in range(pack)], axis=1
        )


def core_kernel(width, block, owners, table, own, *rest):
    gots, cores, (part32, part16) = rest[: width - 1], rest[width - 1 : width - 1 + owners], rest[-2:]
    pack = LANES // block
    total = own[...]
    for got in gots:
        packed = got[...].astype(F32)
        total = total + jnp.concatenate(
            [packed[:, i * block : (i + 1) * block] for i in range(pack)], axis=0
        )
    rows = total.shape[0]
    at = lax.broadcasted_iota(jnp.int32, (rows, block), 0)
    hidden = total.astype(BF16).astype(F32)
    spread = [
        jnp.where((at >= table[0, s]) & (at < table[1, s]), hidden, 0.0) for s in range(owners)
    ]
    lhs = jnp.concatenate(spread, axis=1).astype(BF16)
    rhs = jnp.concatenate([core[...] for core in cores], axis=0)
    part = jnp.dot(lhs, rhs, preferred_element_type=F32)
    part32[...] = part
    part16[...] = part.astype(BF16)


def base_kernel(width, parts, place, tokens, weight, keep, send, tok_buf, w_buf, tok_sem, w_sem):
    x, core = place[1] // CORES, place[1] % CORES
    out_block = keep.shape[2]
    chunks = row_chunks(tok_buf.shape[0], parts)
    order = [(s % width, o) for s in range(1, width + 1) for o in (1, 0)]
    w_copies, tok_copies = [], []
    for i, (shift, other) in enumerate(order):
        block = ((x + shift) % width) * CORES + (core + other) % CORES
        w_copies.append(
            pltpu.make_async_copy(
                weight.at[:, pl.ds(pl.multiple_of(block * out_block, out_block), out_block)],
                w_buf.at[i],
                w_sem.at[i],
            )
        )
    for i, (at, size) in enumerate(chunks):
        tok_copies.append(
            pltpu.make_async_copy(
                tokens.at[pl.ds(at, size)], tok_buf.at[pl.ds(at, size)], tok_sem.at[i]
            )
        )
    w_copies[0].start()
    for copy in tok_copies:
        copy.start()
    for copy in w_copies[1:]:
        copy.start()
    for i, (shift, other) in enumerate(order):
        w_copies[i].wait()
        for j, (at, size) in enumerate(chunks):
            if i == 0:
                tok_copies[j].wait()
            part = jnp.dot(
                tok_buf[at : at + size, :], w_buf[i], preferred_element_type=F32
            )
            if other:
                send[shift, at : at + size, :] = part.astype(BF16)
            else:
                keep[shift, at : at + size, :] = part


def far_kernel(at, size, shift, part32, got_part, up, keep, got_base, out):
    core_out = (part32[...] + got_part[...].astype(F32)).astype(BF16)
    lifted = jnp.dot(core_out, up[...], preferred_element_type=F32)
    out[...] = (keep[0] + got_base[0].astype(F32) + lifted).astype(BF16)


def near_kernel(part32, got_part, up, keep, got_base, out):
    core_out = (part32[...] + got_part[...].astype(F32)).astype(BF16)
    lifted = jnp.dot(core_out, up[...], preferred_element_type=F32)
    out[...] = keep[0] + got_base[0].astype(F32) + lifted


def final_kernel(rows_of, near, *rest):
    gots, out = rest[:-1], rest[-1]
    for i, (at, size) in enumerate(rows_of):
        total = near[at : at + size, :]
        for got in gots[i :: len(rows_of)]:
            total = total + got[...].astype(F32)
        out[at : at + size, :] = total.astype(BF16)


def local(
    tokens, base_weight, down_basis, up_basis, core_bank, request_adapter, request_length, core_slot
):
    rows, depth = tokens.shape
    out_cols, rank = base_weight.shape[1], down_basis.shape[1]
    owners, tensor = lax.axis_size("dp"), lax.axis_size("tensor")
    width = tensor // CORES
    out_block, block = out_cols // tensor, rank // tensor
    per_owner = core_bank.shape[0]
    req_dev = request_length.shape[0] // owners
    place = jnp.stack([lax.axis_index("dp"), lax.axis_index("tensor")]).astype(jnp.int32)

    def pair(a):
        return lax.ppermute(a, "tensor", [(i, i ^ 1) for i in range(tensor)])

    def along_x(a, shift):
        return lax.ppermute(
            a, "tensor", [(i, (i + shift * CORES) % tensor) for i in range(tensor)]
        )

    def along_dp(a, shift):
        return lax.ppermute(a, "dp", [(i, (i + shift) % owners) for i in range(owners)])

    ups = [up_basis] + [along_x(up_basis, -s) for s in range(1, width)]

    parts = 4
    outs = pl.pallas_call(
        functools.partial(
            hidden_kernel, (owners, req_dev, per_owner, width, block, parts)
        ),
        out_shape=[jax.ShapeDtypeStruct((block, rank), BF16)] * owners
        + [
            jax.ShapeDtypeStruct((rows, width * block), BF16),
            jax.ShapeDtypeStruct((rows, width * block), F32),
            jax.ShapeDtypeStruct((2, owners), jnp.int32),
        ],
        in_specs=[SMEM] * 4 + [ANY] * 3,
        out_specs=[VMEM] * (owners + 2) + [SMEM],
        scratch_shapes=[
            pltpu.VMEM((rows, depth), BF16),
            pltpu.VMEM((depth, rank), BF16),
            pltpu.SemaphoreType.DMA((parts,)),
            pltpu.SemaphoreType.DMA,
            pltpu.SemaphoreType.DMA((owners,)),
        ],
        compiler_params=params(),
        cost_estimate=pl.CostEstimate(
            flops=2 * rows * depth * rank, bytes_accessed=2 * depth * (rows + rank), transcendentals=0
        ),
        name="hidden",
    )(place, request_adapter, request_length, core_slot, core_bank, tokens, down_basis)
    picks, (send, keep, table) = outs[:owners], outs[owners:]
    got = pair(send)
    cores = [picks[0]] + [along_dp(picks[s], s) for s in range(1, owners)]

    pack = LANES // block
    outs = pl.pallas_call(
        functools.partial(chip_kernel, width, block),
        out_shape=[jax.ShapeDtypeStruct((rows // pack, LANES), BF16)] * (width - 1)
        + [jax.ShapeDtypeStruct((rows, block), F32)],
        in_specs=[SMEM, VMEM, VMEM],
        out_specs=[VMEM] * width,
        compiler_params=params(),
        name="chip_sum",
    )(place, keep, got)
    hidden_gots = [along_x(outs[s - 1], s) for s in range(1, width)]

    keep_base, send_base = pl.pallas_call(
        functools.partial(base_kernel, width, parts),
        out_shape=[
            jax.ShapeDtypeStruct((width, rows, out_block), F32),
            jax.ShapeDtypeStruct((width, rows, out_block), BF16),
        ],
        in_specs=[SMEM] + [ANY] * 2,
        out_specs=[VMEM] * 2,
        scratch_shapes=[
            pltpu.VMEM((rows, depth), BF16),
            pltpu.VMEM((tensor, depth, out_block), BF16),
            pltpu.SemaphoreType.DMA((parts,)),
            pltpu.SemaphoreType.DMA((tensor,)),
        ],
        compiler_params=params(),
        cost_estimate=pl.CostEstimate(
            flops=2 * rows * depth * out_cols,
            bytes_accessed=2 * depth * (rows + out_cols) + 6 * width * rows * out_block,
            transcendentals=0,
        ),
        name="base",
    )(place, tokens, base_weight)
    got_base = pair(send_base)

    part32, part16 = pl.pallas_call(
        functools.partial(core_kernel, width, block, owners),
        out_shape=[
            jax.ShapeDtypeStruct((rows, rank), F32),
            jax.ShapeDtypeStruct((rows, rank), BF16),
        ],
        in_specs=[SMEM] + [VMEM] * (width + owners),
        out_specs=[VMEM] * 2,
        compiler_params=params(),
        name="core_product",
    )(table, outs[-1], *hidden_gots, *cores)
    got_part = pair(part16)

    halves = 2
    size = rows // halves
    far_gots = []
    for shift in range(1, width):
        for i in range(halves):
            at_rows = pl.BlockSpec((size, rank), functools.partial(lambda i, g: (i, 0), i))
            at_block = pl.BlockSpec(
                (1, size, out_block), functools.partial(lambda s, i, g: (s, i, 0), shift, i)
            )
            far = pl.pallas_call(
                functools.partial(far_kernel, i * size, size, shift),
                grid=(1,),
                out_shape=jax.ShapeDtypeStruct((size, out_block), BF16),
                in_specs=[
                    at_rows,
                    at_rows,
                    pl.BlockSpec((rank, out_block), lambda g: (0, 0)),
                    at_block,
                    at_block,
                ],
                out_specs=pl.BlockSpec((size, out_block), lambda g: (0, 0)),
                compiler_params=params(),
                name="far",
            )(part32, got_part, ups[shift], keep_base, got_base)
            far_gots.append(along_x(far, shift))

    near_block = pl.BlockSpec((1, rows, out_block), lambda g: (0, 0, 0))
    whole_rows = pl.BlockSpec((rows, rank), lambda g: (0, 0))
    near = pl.pallas_call(
        near_kernel,
        grid=(1,),
        out_shape=jax.ShapeDtypeStruct((rows, out_block), F32),
        in_specs=[
            whole_rows,
            whole_rows,
            pl.BlockSpec((rank, out_block), lambda g: (0, 0)),
            near_block,
            near_block,
        ],
        out_specs=pl.BlockSpec((rows, out_block), lambda g: (0, 0)),
        compiler_params=params(),
        name="near",
    )(part32, got_part, up_basis, keep_base, got_base)

    return pl.pallas_call(
        functools.partial(final_kernel, row_chunks(rows, halves)),
        out_shape=jax.ShapeDtypeStruct((rows, out_block), BF16),
        in_specs=[VMEM] * (1 + len(far_gots)),
        out_specs=VMEM,
        compiler_params=params(),
        name="final",
    )(near, *far_gots)


def solution(mesh):
    in_specs = (
        P(("group", "dp"), "tensor"),
        P("tensor", None),
        P("tensor", None),
        P(None, "tensor"),
        P("dp", "tensor", None),
        P("group"),
        P("group"),
        P("group"),
    )
    out_specs = P(("group", "dp"), "tensor")
    return jax.shard_map(local, mesh=mesh, in_specs=in_specs, out_specs=out_specs, check_vma=False)
```

```python
import functools

import jax
import jax.numpy as jnp
from jax import lax
from jax.experimental import pallas as pl
from jax.experimental.pallas import tpu as pltpu
from jax.sharding import PartitionSpec as P

F32 = jnp.float32
BF16 = jnp.bfloat16
CORES = 2
MIB = 1024 * 1024

ANY = pl.BlockSpec(memory_space=pl.ANY)
SMEM = pl.BlockSpec(memory_space=pltpu.SMEM)
VMEM = pl.BlockSpec(memory_space=pltpu.VMEM)


def params(mib=8):
    return pltpu.CompilerParams(vmem_limit_bytes=mib * MIB)


def cost(flops, read):
    return pl.CostEstimate(flops=flops, bytes_accessed=read, transcendentals=0)


def ordered(arrays, *after):
    count = len(arrays)
    return pl.pallas_call(
        lambda *refs: None,
        out_shape=[jax.ShapeDtypeStruct(a.shape, a.dtype) for a in arrays],
        in_specs=[ANY] * (count + len(after)),
        out_specs=[ANY] * count,
        input_output_aliases={i: i for i in range(count)},
        compiler_params=params(1),
        cost_estimate=cost(0, 0),
        name="ordered",
    )(*arrays, *after)


def pick_kernel(sizes, adapters, lengths, slots, bank, after, *rest):
    owners, req_dev, per_owner = sizes
    picks, (table, sem, int_sem) = rest[:owners], rest[owners : owners + 3]
    copies = [
        pltpu.make_async_copy(a, b, int_sem.at[i])
        for i, (a, b) in enumerate(zip((adapters, lengths, slots), rest[owners + 3 :]))
    ]
    for copy in copies:
        copy.start()
    for copy in copies:
        copy.wait()
    adapters, lengths, slots = rest[owners + 3 :]
    me = lax.axis_index("dp")
    copies = []
    for shift in range(owners):
        home = (me + shift) % owners
        index = jnp.int32(0)
        for q in range(req_dev):
            slot = slots[adapters[home * req_dev + q]]
            index = jnp.where(slot // per_owner == me, slot % per_owner, index)
        copy = pltpu.make_async_copy(bank.at[index], picks[shift], sem.at[shift])
        copy.start()
        copies.append(copy)
    for shift in range(owners):
        table[0, shift] = 0
        table[1, shift] = 0
    start = jnp.int32(0)
    for q in range(req_dev):
        owner = slots[adapters[me * req_dev + q]] // per_owner
        shift = (me - owner + owners) % owners
        end = start + lengths[me * req_dev + q]
        table[0, shift] = start
        table[1, shift] = end
        start = end
    for copy in copies:
        copy.wait()


def pack_kernel(owners, *refs):
    far, out = refs[owners], refs[-1]
    cols = far.shape[2]
    block, rank = refs[0].shape
    for s in range(owners):
        for at in range(0, rank, cols):
            out[pl.ds((s * (rank // cols) + at // cols) * block, block), :] = refs[s][:, at : at + cols]
    first = owners * block * rank // cols
    rows = far.shape[1]
    for i in range(far.shape[0]):
        out[pl.ds(first + i * rows, rows), :] = far[i]


def sum_kernel(keep, *rest):
    gots, out = rest[:-1], rest[-1]
    total = keep[...]
    for got in gots:
        total = total + got[: total.shape[0], :].astype(F32)
    out[...] = total


def block_product(width, shift, other, tokens, weight):
    me = lax.axis_index("tensor")
    x, core = me // CORES, me % CORES
    out_block = weight.shape[1] // (width * CORES)
    block = ((x + shift) % width) * CORES + (core + other) % CORES
    columns = pl.ds(pl.multiple_of(block * out_block, out_block), out_block)
    return jnp.dot(tokens[...], weight[:, columns], preferred_element_type=F32)


def far_base_kernel(width, tokens, weight, after, send, keep):
    for shift in range(1, width):
        send[shift - 1] = block_product(width, shift, 1, tokens, weight).astype(BF16)
        keep[shift - 1] = block_product(width, shift, 0, tokens, weight)


def near_base_kernel(width, tokens, weight, after, send, keep):
    send[...] = block_product(width, 0, 1, tokens, weight)
    keep[...] = block_product(width, 0, 0, tokens, weight)


def far_kernel(width, halves, table, hidden, got_hidden, mine, others, *rest):
    ups, keep, rest = rest[: width - 1], rest[width - 1], rest[width + 1 :]
    outs, core_out, rhs = rest[:-2], rest[-2], rest[-1]
    core = lax.axis_index("tensor") % CORES
    owners = table.shape[1]
    rank, cols = core_out.shape[1], outs[0].shape[1]
    block = hidden.shape[1] // CORES
    for s in range(owners):
        for packed, at in ((mine, core), (others, 1 - core)):
            to = pl.ds(pl.multiple_of((s * CORES + at) * block, block), block)
            for i in range(rank // cols):
                rhs[to, i * cols : (i + 1) * cols] = packed[
                    pl.ds((s * (rank // cols) + i) * block, block), :
                ]
    total = (hidden[...] + got_hidden[...]).astype(BF16).astype(F32)
    row = lax.broadcasted_iota(jnp.int32, total.shape, 0)
    lhs = jnp.concatenate(
        [
            jnp.where((row >= table[0, s]) & (row < table[1, s]), total, 0.0).astype(BF16)
            for s in range(owners)
        ],
        axis=1,
    )
    part = jnp.dot(lhs, rhs[...], preferred_element_type=F32).astype(BF16)
    core_out[...] = part
    rows = part.shape[0]
    size = rows // halves
    first = owners * block * rank // cols
    for i in range(width - 1):
        up = jnp.concatenate(
            [ups[i][pl.ds(at, rank), :] for at in range(rows, ups[i].shape[0], rank)], axis=1
        )
        lifted = jnp.dot(part, up, preferred_element_type=F32)
        got = others[pl.ds(first + i * rows, rows), :].astype(F32)
        sent = (keep[i] + got + lifted).astype(BF16)
        for j in range(halves):
            outs[i * halves + j][...] = sent[j * size : (j + 1) * size]


def near_kernel(up, keep, got, part, out):
    lifted = jnp.dot(part[...], up[...], preferred_element_type=F32)
    out[...] = keep[...] + got[...] + lifted


def final_kernel(halves, near, *rest):
    gots, out = rest[:-1], rest[-1]
    size = near.shape[0] // halves
    for i in range(halves):
        rows = pl.ds(i * size, size)
        total = near[rows, :]
        for got in gots[i::halves]:
            total = total + got[...].astype(F32)
        out[rows, :] = total.astype(BF16)


def local(
    tokens, base_weight, down_basis, up_basis, core_bank, request_adapter, request_length, core_slot
):
    rows, depth = tokens.shape
    out_cols, rank = base_weight.shape[1], down_basis.shape[1]
    owners, tensor = lax.axis_size("dp"), lax.axis_size("tensor")
    width = tensor // CORES
    out_block, block = out_cols // tensor, rank // tensor
    cols = CORES * block
    per_owner = core_bank.shape[0]
    req_dev = request_length.shape[0] // owners
    def pair(a):
        return lax.ppermute(a, "tensor", [(i, i ^ 1) for i in range(tensor)])

    def along_x(a, shift):
        return lax.ppermute(
            a, "tensor", [(i, (i + shift * CORES) % tensor) for i in range(tensor)]
        )

    def along_dp(a, shift):
        return lax.ppermute(a, "dp", [(i, (i + shift) % owners) for i in range(owners)])

    up_parts = [up_basis[:, at : at + cols] for at in range(0, out_block, cols)]

    chip = lax.axis_index("tensor") // CORES
    part = jnp.dot(tokens, down_basis, preferred_element_type=F32)
    keep = lax.dynamic_slice_in_dim(part, chip * cols, cols, axis=1)
    gots = []
    for shift in range(1, width):
        at = (chip + shift) % width * cols
        send = lax.dynamic_slice_in_dim(part, at, cols, axis=1).astype(BF16)
        gots.append(along_x(jnp.concatenate([send] + up_parts, axis=0), shift))

    outs = pl.pallas_call(
        functools.partial(pick_kernel, (owners, req_dev, per_owner)),
        out_shape=[jax.ShapeDtypeStruct((block, rank), BF16)] * owners
        + [jax.ShapeDtypeStruct((2, owners), jnp.int32)],
        in_specs=[ANY] * 5,
        out_specs=[VMEM] * owners + [SMEM],
        scratch_shapes=[
            pltpu.SemaphoreType.DMA((owners,)),
            pltpu.SemaphoreType.DMA((3,)),
            pltpu.SMEM(request_adapter.shape, jnp.int32),
            pltpu.SMEM(request_length.shape, jnp.int32),
            pltpu.SMEM(core_slot.shape, jnp.int32),
        ],
        compiler_params=params(38),
        cost_estimate=cost(0, 8 * MIB),
        name="pick",
    )(request_adapter, request_length, core_slot, core_bank, keep)
    table = outs[-1]
    mine = [outs[0]] + [along_dp(outs[s], s) for s in range(1, owners)]

    hidden = pl.pallas_call(
        sum_kernel,
        out_shape=jax.ShapeDtypeStruct((rows, cols), F32),
        in_specs=[VMEM] * width,
        out_specs=VMEM,
        compiler_params=params(),
        cost_estimate=cost(0, rows * cols * 10),
        name="hidden_sum",
    )(keep, *gots)
    got_hidden = pair(hidden)

    def base(kernel, dtypes, lead, after, name):
        shape = lead + (rows, out_block)
        blocks = CORES * (lead[0] if lead else 1)
        return pl.pallas_call(
            functools.partial(kernel, width),
            out_shape=[jax.ShapeDtypeStruct(shape, dtype) for dtype in dtypes],
            in_specs=[VMEM] * 2 + [ANY],
            out_specs=[VMEM] * 2,
            compiler_params=params(),
            cost_estimate=cost(
                2 * rows * depth * out_block * blocks, 2 * depth * (rows + out_block * blocks)
            ),
            name=name,
        )(tokens, base_weight, after)

    far_send, far_keep = base(far_base_kernel, (BF16, F32), (width - 1,), outs[0], "far_base")

    packed = pl.pallas_call(
        functools.partial(pack_kernel, owners),
        out_shape=jax.ShapeDtypeStruct(
            (owners * block * rank // out_block + (width - 1) * rows, out_block), BF16
        ),
        in_specs=[VMEM] * (owners + 1),
        out_specs=VMEM,
        compiler_params=params(),
        cost_estimate=cost(0, 0),
        name="pack",
    )(*mine, far_send)
    got_packed = pair(packed)
    near_send, near_keep = base(near_base_kernel, (F32, F32), (), packed, "near_base")

    halves = 2
    size = rows // halves
    outs = pl.pallas_call(
        functools.partial(far_kernel, width, halves),
        out_shape=[jax.ShapeDtypeStruct((size, out_block), BF16)] * (halves * (width - 1))
        + [jax.ShapeDtypeStruct((rows, rank), BF16)],
        in_specs=[SMEM] + [VMEM] * (4 + width) + [ANY],
        out_specs=[VMEM] * (halves * (width - 1) + 1),
        scratch_shapes=[pltpu.VMEM((owners * cols, rank), BF16)],
        compiler_params=params(),
        cost_estimate=cost(2 * rows * (owners * cols * rank + rank * out_block), rows * out_block * 10),
        name="far",
    )(table, hidden, got_hidden, packed, got_packed, *gots[::-1], far_keep, near_keep)
    core_out = outs[-1]
    order = [along_x(outs[i], i // halves + 1) for i in range(halves * (width - 1))]

    (near_send,) = ordered([near_send], core_out)
    near_got = pair(near_send)
    near = pl.pallas_call(
        near_kernel,
        out_shape=jax.ShapeDtypeStruct((rows, out_block), F32),
        in_specs=[VMEM] * 4,
        out_specs=VMEM,
        compiler_params=params(),
        cost_estimate=cost(2 * rows * rank * out_block, rows * out_block * 12),
        name="near",
    )(up_basis, near_keep, near_got, core_out)

    return pl.pallas_call(
        functools.partial(final_kernel, halves),
        out_shape=jax.ShapeDtypeStruct((rows, out_block), BF16),
        in_specs=[VMEM] * (1 + len(order)),
        out_specs=VMEM,
        compiler_params=params(),
        cost_estimate=cost(0, rows * out_block * 8),
        name="final",
    )(near, *order)


def solution(mesh):
    in_specs = (
        P(("group", "dp"), "tensor"),
        P("tensor", None),
        P("tensor", None),
        P(None, "tensor"),
        P("dp", "tensor", None),
        P("group"),
        P("group"),
        P("group"),
    )
    out_specs = P(("group", "dp"), "tensor")
    return jax.shard_map(local, mesh=mesh, in_specs=in_specs, out_specs=out_specs, check_vma=False)
```

```python
import functools
import math

import jax
import jax.numpy as jnp
from jax import lax
from jax.experimental import pallas as pl
from jax.experimental.pallas import tpu as pltpu
from jax.sharding import PartitionSpec as P

F32 = jnp.float32
BF16 = jnp.bfloat16
CORES = 2
MIB = 1024 * 1024

ANY = pl.BlockSpec(memory_space=pl.ANY)
VMEM = pl.BlockSpec(memory_space=pltpu.VMEM)


def params(mib=8):
    return pltpu.CompilerParams(vmem_limit_bytes=mib * MIB)


def cost(flops, read):
    return pl.CostEstimate(flops=flops, bytes_accessed=read, transcendentals=0)


def ordered(arrays, *after, read=0):
    count = len(arrays)
    return pl.pallas_call(
        lambda *refs: None,
        out_shape=[jax.ShapeDtypeStruct(a.shape, a.dtype) for a in arrays],
        in_specs=[ANY] * (count + len(after)),
        out_specs=[ANY] * count,
        input_output_aliases={i: i for i in range(count)},
        compiler_params=params(1),
        cost_estimate=cost(0, read),
        name="ordered",
    )(*arrays, *after)


def split_kernel(width, part, up, *rest):
    sends, keep = rest[:-1], rest[-1]
    x = lax.axis_index("tensor") // CORES
    rows, cols = keep.shape
    rank, out_block = up.shape
    pieces = [part[:, i * cols : (i + 1) * cols] for i in range(width)]

    def piece(index):
        out = pieces[0]
        for i in range(1, width):
            out = jnp.where(index == i, pieces[i], out)
        return out

    keep[...] = piece(x)
    for shift in range(1, width):
        send = sends[shift - 1]
        send[:rows, :] = piece((x + shift) % width).astype(BF16)
        for i in range(out_block // cols):
            send[pl.ds(rows + i * rank, rank), :] = up[:, i * cols : (i + 1) * cols]


def pick_kernel(sizes, adapters, lengths, slots, bank, after, *rest):
    owners, req_dev, per_owner = sizes
    picks, (table, sem, int_sem) = rest[:owners], rest[owners : owners + 3]
    copies = [
        pltpu.make_async_copy(a, b, int_sem.at[i])
        for i, (a, b) in enumerate(zip((adapters, lengths, slots), rest[owners + 3 :]))
    ]
    for copy in copies:
        copy.start()
    for copy in copies:
        copy.wait()
    adapters, lengths, slots = rest[owners + 3 :]
    me = lax.axis_index("dp")
    copies = []
    for shift in range(owners):
        home = me ^ shift
        index = jnp.int32(0)
        for q in range(req_dev):
            slot = slots[adapters[home * req_dev + q]]
            index = jnp.where(slot // per_owner == me, slot % per_owner, index)
        copy = pltpu.make_async_copy(bank.at[index], picks[shift], sem.at[shift])
        copy.start()
        copies.append(copy)
    start = jnp.int32(0)
    at = lax.broadcasted_iota(jnp.int32, table.shape, 0)
    lane = lax.broadcasted_iota(jnp.int32, table.shape, 1)
    bounds = jnp.zeros(table.shape, jnp.int32)
    for q in range(req_dev):
        shift = (slots[adapters[me * req_dev + q]] // per_owner) ^ me
        end = start + lengths[me * req_dev + q]
        bounds = jnp.where(at == shift, jnp.where(lane == 0, start, end), bounds)
        start = end
    table[...] = bounds
    for copy in copies:
        copy.wait()


def pack_kernel(order, *refs):
    out = refs[-1]
    for i, s in enumerate(order):
        out[s] = refs[i][...]


def sum_kernel(keep, *rest):
    gots, (out, send) = rest[:-2], rest[-2:]
    total = keep[...]
    for got in gots:
        total = total + got[: total.shape[0], :].astype(F32)
    out[...] = total
    send[...] = total.astype(BF16)


def block_product(width, shift, other, tokens, weight):
    me = lax.axis_index("tensor")
    x, core = me // CORES, me % CORES
    out_block = weight.shape[1] // (width * CORES)
    block = ((x + shift) % width) * CORES + (core + other) % CORES
    columns = pl.ds(pl.multiple_of(block * out_block, out_block), out_block)
    return jnp.dot(tokens[...], weight[:, columns], preferred_element_type=F32)


def far_base_kernel(width, owners, tokens, weight, table, keep, mask, *sends):
    rows, cols = tokens.shape[0], mask.shape[1] // owners
    row = lax.broadcasted_iota(jnp.int32, (rows, cols), 0)
    for s in range(owners):
        inside = (row >= table[s : s + 1, 0:1]) & (row < table[s : s + 1, 1:2])
        mask[:, s * cols : (s + 1) * cols] = jnp.where(inside, 1.0, 0.0).astype(BF16)
    size = sends[0].shape[1]
    for shift in range(1, width):
        other = block_product(width, shift, 1, tokens, weight).astype(BF16)
        for i, send in enumerate(sends):
            send[shift - 1] = other[i * size : (i + 1) * size]
        keep[shift - 1] = block_product(width, shift, 0, tokens, weight)


def near_base_kernel(width, tokens, weight, after, keep, *sends):
    other = block_product(width, 0, 1, tokens, weight).astype(BF16)
    size = sends[0].shape[0]
    for i, send in enumerate(sends):
        send[...] = other[i * size : (i + 1) * size]
    keep[...] = block_product(width, 0, 0, tokens, weight)


def far_kernel(width, halves, mask, hidden, got_hidden, mine, others, *rest):
    ups, keep, rest = rest[: width - 1], rest[width - 1], rest[width:]
    gots, rest = rest[: -halves * (width - 1) - 2], rest[-halves * (width - 1) - 2 :]
    outs, core_out, rhs = rest[:-2], rest[-2], rest[-1]
    core = lax.axis_index("tensor") % CORES
    owners = mask.shape[1] // hidden.shape[1]
    rank = core_out.shape[1]
    block = hidden.shape[1] // CORES
    owners = mask.shape[1] // hidden.shape[1]
    for s in range(owners):
        for cores, at in ((mine, core), (others, 1 - core)):
            rhs[pl.ds(pl.multiple_of((s * CORES + at) * block, block), block), :] = cores[s]
    total = (hidden[...] + got_hidden[...].astype(F32)).astype(BF16)
    lhs = jnp.concatenate([total] * owners, axis=1) * mask[...]
    part = jnp.dot(lhs, rhs[...], preferred_element_type=F32).astype(BF16)
    core_out[...] = part
    rows = part.shape[0]
    size = rows // halves
    for i in range(width - 1):
        up = jnp.concatenate(
            [ups[i][pl.ds(at, rank), :] for at in range(rows, ups[i].shape[0], rank)], axis=1
        )
        lifted = jnp.dot(part, up, preferred_element_type=F32)
        got = jnp.concatenate([a[i] for a in gots], axis=0).astype(F32)
        sent = (keep[i] + got + lifted).astype(BF16)
        for j in range(halves):
            outs[i * halves + j][...] = sent[j * size : (j + 1) * size]


def near_kernel(up, keep, part, *rest):
    gots, out = rest[:-1], rest[-1]
    lifted = jnp.dot(part[...], up[...], preferred_element_type=F32)
    got = jnp.concatenate([a[...] for a in gots], axis=0).astype(F32)
    out[...] = keep[...] + got + lifted


def final_kernel(halves, near, *rest):
    gots, out = rest[:-1], rest[-1]
    size = near.shape[0] // halves
    for i in range(halves):
        rows = pl.ds(i * size, size)
        total = near[rows, :]
        for got in gots[i::halves]:
            total = total + got[...].astype(F32)
        out[rows, :] = total.astype(BF16)


def local(
    tokens, base_weight, down_basis, up_basis, core_bank, request_adapter, request_length, core_slot
):
    rows, depth = tokens.shape
    out_cols, rank = base_weight.shape[1], down_basis.shape[1]
    owners, tensor = lax.axis_size("dp"), lax.axis_size("tensor")
    width = tensor // CORES
    out_block, block = out_cols // tensor, rank // tensor
    cols = CORES * block
    per_owner = core_bank.shape[0]
    req_dev = request_length.shape[0] // owners
    def pair(a):
        return lax.ppermute(a, "tensor", [(i, i ^ 1) for i in range(tensor)])

    def along_x(a, shift):
        return lax.ppermute(
            a, "tensor", [(i, (i + shift * CORES) % tensor) for i in range(tensor)]
        )

    def along_dp(a, shift):
        return lax.ppermute(a, "dp", [(i, i ^ shift) for i in range(owners)])

    part = jnp.dot(tokens, down_basis, preferred_element_type=F32)
    outs = pl.pallas_call(
        functools.partial(split_kernel, width),
        out_shape=[jax.ShapeDtypeStruct((rows + rank * out_block // cols, cols), BF16)] * (width - 1)
        + [jax.ShapeDtypeStruct((rows, cols), F32)],
        in_specs=[VMEM] * 2,
        out_specs=[VMEM] * width,
        compiler_params=params(),
        cost_estimate=cost(0, 0),
        name="split",
    )(part, up_basis)
    keep = outs[-1]
    gots = [along_x(outs[s - 1], s) for s in range(1, width)]

    outs = pl.pallas_call(
        functools.partial(pick_kernel, (owners, req_dev, per_owner)),
        out_shape=[jax.ShapeDtypeStruct((block, rank), BF16)] * owners
        + [jax.ShapeDtypeStruct((max(owners, 8), 128), jnp.int32)],
        in_specs=[ANY] * 5,
        out_specs=[VMEM] * (owners + 1),
        scratch_shapes=[
            pltpu.SemaphoreType.DMA((owners,)),
            pltpu.SemaphoreType.DMA((3,)),
            pltpu.SMEM(request_adapter.shape, jnp.int32),
            pltpu.SMEM(request_length.shape, jnp.int32),
            pltpu.SMEM(core_slot.shape, jnp.int32),
        ],
        compiler_params=params(38),
        cost_estimate=cost(0, 2 * MIB),
        name="pick",
    )(request_adapter, request_length, core_slot, core_bank, keep)
    table = outs[-1]
    picks = ordered(outs[:-1], read=30 * MIB)
    order = sorted(range(1, owners), key=lambda s: -s.bit_length())
    mine = [picks[0]] + [along_dp(picks[s], s) for s in order]

    hidden, hidden_send = pl.pallas_call(
        sum_kernel,
        out_shape=[jax.ShapeDtypeStruct((rows, cols), dtype) for dtype in (F32, BF16)],
        in_specs=[VMEM] * width,
        out_specs=[VMEM] * 2,
        compiler_params=params(),
        cost_estimate=cost(0, rows * cols * 10),
        name="hidden_sum",
    )(keep, *gots)
    got_hidden = pair(hidden_send)

    def base(kernel, shapes, after, name):
        blocks = math.prod(shapes[0].shape[:-2]) * CORES
        return pl.pallas_call(
            kernel,
            out_shape=shapes,
            in_specs=[VMEM] * 3,
            out_specs=[VMEM] * len(shapes),
            compiler_params=params(),
            cost_estimate=cost(
                2 * rows * depth * out_block * blocks, 2 * depth * (rows + out_block * blocks)
            ),
            name=name,
        )(tokens, base_weight, after)

    parts = 2
    far_keep, mask, *far_send = base(
        functools.partial(far_base_kernel, width, owners),
        [
            jax.ShapeDtypeStruct((width - 1, rows, out_block), F32),
            jax.ShapeDtypeStruct((rows, owners * cols), BF16),
        ]
        + [jax.ShapeDtypeStruct((width - 1, rows // parts, out_block), BF16)] * parts,
        ordered([table], picks[0])[0],
        "far_base",
    )

    near_keep, *near_send = base(
        functools.partial(near_base_kernel, width),
        [jax.ShapeDtypeStruct((rows, out_block), F32)]
        + [jax.ShapeDtypeStruct((rows // parts, out_block), BF16)] * parts,
        ordered([hidden], far_keep)[0],
        "near_base",
    )

    packed = pl.pallas_call(
        functools.partial(pack_kernel, [0] + order),
        out_shape=jax.ShapeDtypeStruct((owners, block, rank), BF16),
        in_specs=[VMEM] * owners + [ANY],
        out_specs=VMEM,
        compiler_params=params(),
        cost_estimate=cost(0, 0),
        name="pack",
    )(*mine, near_keep)
    got_packed = pair(packed)
    far_got = [pair(a) for a in far_send]

    halves = 1
    size = rows // halves
    outs = pl.pallas_call(
        functools.partial(far_kernel, width, halves),
        out_shape=[jax.ShapeDtypeStruct((size, out_block), BF16)] * (halves * (width - 1))
        + [jax.ShapeDtypeStruct((rows, rank), BF16)],
        in_specs=[VMEM] * (5 + width + parts),
        out_specs=[VMEM] * (halves * (width - 1) + 1),
        scratch_shapes=[pltpu.VMEM((owners * cols, rank), BF16)],
        compiler_params=params(),
        cost_estimate=cost(2 * rows * (owners * cols * rank + rank * out_block), rows * out_block * 10),
        name="far",
    )(mask, hidden, got_hidden, packed, got_packed, *gots[::-1], far_keep, *far_got)
    core_out = outs[-1]
    far_gots = [along_x(outs[i], i // halves + 1) for i in range(halves * (width - 1))]

    near_got = [pair(a) for a in ordered(near_send, core_out)]
    near = pl.pallas_call(
        near_kernel,
        out_shape=jax.ShapeDtypeStruct((rows, out_block), F32),
        in_specs=[VMEM] * (3 + parts),
        out_specs=VMEM,
        compiler_params=params(),
        cost_estimate=cost(2 * rows * rank * out_block, rows * out_block * 12),
        name="near",
    )(up_basis, near_keep, core_out, *near_got)

    return pl.pallas_call(
        functools.partial(final_kernel, halves),
        out_shape=jax.ShapeDtypeStruct((rows, out_block), BF16),
        in_specs=[VMEM] * (1 + len(far_gots)),
        out_specs=VMEM,
        compiler_params=params(),
        cost_estimate=cost(0, rows * out_block * 8),
        name="final",
    )(near, *far_gots)


def solution(mesh):
    in_specs = (
        P(("group", "dp"), "tensor"),
        P("tensor", None),
        P("tensor", None),
        P(None, "tensor"),
        P("dp", "tensor", None),
        P("group"),
        P("group"),
        P("group"),
    )
    out_specs = P(("group", "dp"), "tensor")
    return jax.shard_map(local, mesh=mesh, in_specs=in_specs, out_specs=out_specs, check_vma=False)
```

```python
import functools

import jax
import jax.numpy as jnp
from jax import lax
from jax.experimental import pallas as pl
from jax.experimental.pallas import tpu as pltpu
from jax.sharding import PartitionSpec as P

F32 = jnp.float32
BF16 = jnp.bfloat16
CORES = 2
MIB = 1024 * 1024

ANY = pl.BlockSpec(memory_space=pl.ANY)
VMEM = pl.BlockSpec(memory_space=pltpu.VMEM)


def params(mib=8):
    return pltpu.CompilerParams(vmem_limit_bytes=mib * MIB)


def cost(flops, read):
    return pl.CostEstimate(flops=flops, bytes_accessed=read, transcendentals=0)


def ordered(arrays, *after, read=0):
    count = len(arrays)
    return pl.pallas_call(
        lambda *refs: None,
        out_shape=[jax.ShapeDtypeStruct(a.shape, a.dtype) for a in arrays],
        in_specs=[ANY] * (count + len(after)),
        out_specs=[ANY] * count,
        input_output_aliases={i: i for i in range(count)},
        compiler_params=params(1),
        cost_estimate=cost(0, read),
        name="ordered",
    )(*arrays, *after)


def split_kernel(width, part, up, *rest):
    sends, keep = rest[:-1], rest[-1]
    x = lax.axis_index("tensor") // CORES
    rows, cols = keep.shape
    rank, out_block = up.shape
    pieces = [part[:, i * cols : (i + 1) * cols] for i in range(width)]

    def piece(index):
        out = pieces[0]
        for i in range(1, width):
            out = jnp.where(index == i, pieces[i], out)
        return out

    keep[...] = piece(x)
    for shift in range(1, width):
        send = sends[shift - 1]
        send[:rows, :] = piece((x + shift) % width).astype(BF16)
        for i in range(out_block // cols):
            send[pl.ds(rows + i * rank, rank), :] = up[:, i * cols : (i + 1) * cols]


def pick_kernel(sizes, adapters, lengths, slots, bank, after, *rest):
    owners, req_dev, per_owner = sizes
    picks, (table, sem, int_sem) = rest[:owners], rest[owners : owners + 3]
    copies = [
        pltpu.make_async_copy(a, b, int_sem.at[i])
        for i, (a, b) in enumerate(zip((adapters, lengths, slots), rest[owners + 3 :]))
    ]
    for copy in copies:
        copy.start()
    for copy in copies:
        copy.wait()
    adapters, lengths, slots = rest[owners + 3 :]
    me = lax.axis_index("dp")
    copies = []
    for shift in range(owners):
        home = me ^ shift
        index = jnp.int32(0)
        for q in range(req_dev):
            slot = slots[adapters[home * req_dev + q]]
            index = jnp.where(slot // per_owner == me, slot % per_owner, index)
        copy = pltpu.make_async_copy(bank.at[index], picks[shift], sem.at[shift])
        copy.start()
        copies.append(copy)
    start = jnp.int32(0)
    at = lax.broadcasted_iota(jnp.int32, table.shape, 0)
    lane = lax.broadcasted_iota(jnp.int32, table.shape, 1)
    bounds = jnp.zeros(table.shape, jnp.int32)
    for q in range(req_dev):
        shift = (slots[adapters[me * req_dev + q]] // per_owner) ^ me
        end = start + lengths[me * req_dev + q]
        bounds = jnp.where(at == shift, jnp.where(lane == 0, start, end), bounds)
        start = end
    table[...] = bounds
    for copy in copies:
        copy.wait()


def pack_kernel(order, *refs):
    out = refs[-1]
    for i, s in enumerate(order):
        out[s] = refs[i][...]


def sum_kernel(keep, *rest):
    gots, (out, send) = rest[:-2], rest[-2:]
    total = keep[...]
    for got in gots:
        total = total + got[: total.shape[0], :].astype(F32)
    out[...] = total
    send[...] = total.astype(BF16)


def block_product(width, shift, other, tokens, weight):
    me = lax.axis_index("tensor")
    x, core = me // CORES, me % CORES
    out_block = weight.shape[1] // (width * CORES)
    block = ((x + shift) % width) * CORES + (core + other) % CORES
    columns = pl.ds(pl.multiple_of(block * out_block, out_block), out_block)
    return jnp.dot(tokens[...], weight[:, columns], preferred_element_type=F32)


def far_base_kernel(width, tokens, weight, after, keep, *sends):
    size = sends[0].shape[1]
    for shift in range(1, width):
        other = block_product(width, shift, 1, tokens, weight).astype(BF16)
        for i, send in enumerate(sends):
            send[shift - 1] = other[i * size : (i + 1) * size]
        keep[shift - 1] = block_product(width, shift, 0, tokens, weight)


def near_send_kernel(width, owners, tokens, weight, table, after, mask, *sends):
    rows, cols = tokens.shape[0], mask.shape[1] // owners
    row = lax.broadcasted_iota(jnp.int32, (rows, cols), 0)
    for s in range(owners):
        inside = (row >= table[s : s + 1, 0:1]) & (row < table[s : s + 1, 1:2])
        mask[:, s * cols : (s + 1) * cols] = jnp.where(inside, 1.0, 0.0).astype(BF16)
    other = block_product(width, 0, 1, tokens, weight).astype(BF16)
    size = sends[0].shape[0]
    for i, send in enumerate(sends):
        send[...] = other[i * size : (i + 1) * size]


def near_keep_kernel(width, tokens, weight, after, keep):
    keep[...] = block_product(width, 0, 0, tokens, weight)


def far_kernel(width, halves, mask, hidden, got_hidden, mine, others, *rest):
    ups, keep, rest = rest[: width - 1], rest[width - 1], rest[width:]
    gots, rest = rest[: -halves * (width - 1) - 2], rest[-halves * (width - 1) - 2 :]
    outs, core_out, rhs = rest[:-2], rest[-2], rest[-1]
    core = lax.axis_index("tensor") % CORES
    owners = mask.shape[1] // hidden.shape[1]
    rank = core_out.shape[1]
    block = hidden.shape[1] // CORES
    owners = mask.shape[1] // hidden.shape[1]
    for s in range(owners):
        for cores, at in ((mine, core), (others, 1 - core)):
            rhs[pl.ds(pl.multiple_of((s * CORES + at) * block, block), block), :] = cores[s]
    total = (hidden[...] + got_hidden[...].astype(F32)).astype(BF16)
    lhs = jnp.concatenate([total] * owners, axis=1) * mask[...]
    part = jnp.dot(lhs, rhs[...], preferred_element_type=F32).astype(BF16)
    core_out[...] = part
    rows = part.shape[0]
    size = rows // halves
    for i in range(width - 1):
        up = jnp.concatenate(
            [ups[i][pl.ds(at, rank), :] for at in range(rows, ups[i].shape[0], rank)], axis=1
        )
        lifted = jnp.dot(part, up, preferred_element_type=F32)
        got = jnp.concatenate([a[i] for a in gots], axis=0).astype(F32)
        sent = (keep[i] + got + lifted).astype(BF16)
        for j in range(halves):
            outs[i * halves + j][...] = sent[j * size : (j + 1) * size]


def near_kernel(up, keep, part, *rest):
    gots, out = rest[:-1], rest[-1]
    lifted = jnp.dot(part[...], up[...], preferred_element_type=F32)
    got = jnp.concatenate([a[...] for a in gots], axis=0).astype(F32)
    out[...] = keep[...] + got + lifted


def final_kernel(halves, near, *rest):
    gots, out = rest[:-1], rest[-1]
    size = near.shape[0] // halves
    for i in range(halves):
        rows = pl.ds(i * size, size)
        total = near[rows, :]
        for got in gots[i::halves]:
            total = total + got[...].astype(F32)
        out[rows, :] = total.astype(BF16)


def local(
    tokens, base_weight, down_basis, up_basis, core_bank, request_adapter, request_length, core_slot
):
    rows, depth = tokens.shape
    out_cols, rank = base_weight.shape[1], down_basis.shape[1]
    owners, tensor = lax.axis_size("dp"), lax.axis_size("tensor")
    width = tensor // CORES
    out_block, block = out_cols // tensor, rank // tensor
    cols = CORES * block
    per_owner = core_bank.shape[0]
    req_dev = request_length.shape[0] // owners
    def pair(a):
        return lax.ppermute(a, "tensor", [(i, i ^ 1) for i in range(tensor)])

    def along_x(a, shift):
        return lax.ppermute(
            a, "tensor", [(i, (i + shift * CORES) % tensor) for i in range(tensor)]
        )

    def along_dp(a, shift):
        return lax.ppermute(a, "dp", [(i, i ^ shift) for i in range(owners)])

    part = jnp.dot(tokens, down_basis, preferred_element_type=F32)
    outs = pl.pallas_call(
        functools.partial(split_kernel, width),
        out_shape=[jax.ShapeDtypeStruct((rows + rank * out_block // cols, cols), BF16)] * (width - 1)
        + [jax.ShapeDtypeStruct((rows, cols), F32)],
        in_specs=[VMEM] * 2,
        out_specs=[VMEM] * width,
        compiler_params=params(),
        cost_estimate=cost(0, 0),
        name="split",
    )(part, up_basis)
    keep = outs[-1]
    gots = [along_x(outs[s - 1], s) for s in range(1, width)]

    outs = pl.pallas_call(
        functools.partial(pick_kernel, (owners, req_dev, per_owner)),
        out_shape=[jax.ShapeDtypeStruct((block, rank), BF16)] * owners
        + [jax.ShapeDtypeStruct((max(owners, 8), 128), jnp.int32)],
        in_specs=[ANY] * 5,
        out_specs=[VMEM] * (owners + 1),
        scratch_shapes=[
            pltpu.SemaphoreType.DMA((owners,)),
            pltpu.SemaphoreType.DMA((3,)),
            pltpu.SMEM(request_adapter.shape, jnp.int32),
            pltpu.SMEM(request_length.shape, jnp.int32),
            pltpu.SMEM(core_slot.shape, jnp.int32),
        ],
        compiler_params=params(38),
        cost_estimate=cost(0, 2 * MIB),
        name="pick",
    )(request_adapter, request_length, core_slot, core_bank, keep)
    table = outs[-1]
    picks = ordered(outs[:-1], read=30 * MIB)
    order = sorted(range(1, owners), key=lambda s: -s.bit_length())
    mine = [picks[0]] + [along_dp(picks[s], s) for s in order]

    hidden, hidden_send = pl.pallas_call(
        sum_kernel,
        out_shape=[jax.ShapeDtypeStruct((rows, cols), dtype) for dtype in (F32, BF16)],
        in_specs=[VMEM] * width,
        out_specs=[VMEM] * 2,
        compiler_params=params(),
        cost_estimate=cost(0, rows * cols * 10),
        name="hidden_sum",
    )(keep, *gots)
    got_hidden = pair(hidden_send)

    def base(kernel, shapes, after, name, blocks):
        return pl.pallas_call(
            kernel,
            out_shape=shapes,
            in_specs=[VMEM] * (1 + len(after)) + [ANY],
            out_specs=[VMEM] * len(shapes),
            compiler_params=params(),
            cost_estimate=cost(
                2 * rows * depth * out_block * blocks, 2 * depth * (rows + out_block * blocks)
            ),
            name=name,
        )(tokens, base_weight, *after)

    parts = 2
    far_keep, *far_send = base(
        functools.partial(far_base_kernel, width),
        [jax.ShapeDtypeStruct((width - 1, rows, out_block), F32)]
        + [jax.ShapeDtypeStruct((width - 1, rows // parts, out_block), BF16)] * parts,
        [picks[0]],
        "far_base",
        CORES * (width - 1),
    )
    mask, *near_send = base(
        functools.partial(near_send_kernel, width, owners),
        [jax.ShapeDtypeStruct((rows, owners * cols), BF16)]
        + [jax.ShapeDtypeStruct((rows // parts, out_block), BF16)] * parts,
        [table, ordered([hidden], far_keep, down_basis)[0]],
        "near_send",
        1,
    )

    packed = pl.pallas_call(
        functools.partial(pack_kernel, [0] + order),
        out_shape=jax.ShapeDtypeStruct((owners, block, rank), BF16),
        in_specs=[VMEM] * owners + [ANY],
        out_specs=VMEM,
        compiler_params=params(),
        cost_estimate=cost(0, 0),
        name="pack",
    )(*mine, mask)
    got_packed = pair(packed)
    far_got = [pair(a) for a in far_send]

    halves = 1
    size = rows // halves
    outs = pl.pallas_call(
        functools.partial(far_kernel, width, halves),
        out_shape=[jax.ShapeDtypeStruct((size, out_block), BF16)] * (halves * (width - 1))
        + [jax.ShapeDtypeStruct((rows, rank), BF16)],
        in_specs=[VMEM] * (5 + width + parts),
        out_specs=[VMEM] * (halves * (width - 1) + 1),
        scratch_shapes=[pltpu.VMEM((owners * cols, rank), BF16)],
        compiler_params=params(),
        cost_estimate=cost(2 * rows * (owners * cols * rank + rank * out_block), rows * out_block * 10),
        name="far",
    )(mask, hidden, got_hidden, packed, got_packed, *gots[::-1], far_keep, *far_got)
    core_out = outs[-1]
    far_gots = [along_x(outs[i], i // halves + 1) for i in range(halves * (width - 1))]

    near_got = [pair(a) for a in ordered(near_send, core_out)]
    (near_keep,) = base(
        functools.partial(near_keep_kernel, width),
        [jax.ShapeDtypeStruct((rows, out_block), F32)],
        [core_out],
        "near_keep",
        1,
    )
    near = pl.pallas_call(
        near_kernel,
        out_shape=jax.ShapeDtypeStruct((rows, out_block), F32),
        in_specs=[VMEM] * (3 + parts),
        out_specs=VMEM,
        compiler_params=params(),
        cost_estimate=cost(2 * rows * rank * out_block, rows * out_block * 12),
        name="near",
    )(up_basis, near_keep, core_out, *near_got)

    return pl.pallas_call(
        functools.partial(final_kernel, halves),
        out_shape=jax.ShapeDtypeStruct((rows, out_block), BF16),
        in_specs=[VMEM] * (1 + len(far_gots)),
        out_specs=VMEM,
        compiler_params=params(),
        cost_estimate=cost(0, rows * out_block * 8),
        name="final",
    )(near, *far_gots)


def solution(mesh):
    in_specs = (
        P(("group", "dp"), "tensor"),
        P("tensor", None),
        P("tensor", None),
        P(None, "tensor"),
        P("dp", "tensor", None),
        P("group"),
        P("group"),
        P("group"),
    )
    out_specs = P(("group", "dp"), "tensor")
    return jax.shard_map(local, mesh=mesh, in_specs=in_specs, out_specs=out_specs, check_vma=False)
```

```python
import functools

import jax
import jax.numpy as jnp
from jax import lax
from jax.experimental import pallas as pl
from jax.experimental.pallas import tpu as pltpu
from jax.sharding import PartitionSpec as P

F32 = jnp.float32
BF16 = jnp.bfloat16
CORES = 2
MIB = 1024 * 1024

ANY = pl.BlockSpec(memory_space=pl.ANY)
VMEM = pl.BlockSpec(memory_space=pltpu.VMEM)


def params(mib=8):
    return pltpu.CompilerParams(vmem_limit_bytes=mib * MIB)


def cost(flops, read):
    return pl.CostEstimate(flops=flops, bytes_accessed=read, transcendentals=0)


def ordered(arrays, *after, read=0):
    count = len(arrays)
    return pl.pallas_call(
        lambda *refs: None,
        out_shape=[jax.ShapeDtypeStruct(a.shape, a.dtype) for a in arrays],
        in_specs=[ANY] * (count + len(after)),
        out_specs=[ANY] * count,
        input_output_aliases={i: i for i in range(count)},
        compiler_params=params(1),
        cost_estimate=cost(0, read),
        name="ordered",
    )(*arrays, *after)


def split_kernel(width, part, up, *rest):
    sends, keep = rest[:-1], rest[-1]
    x = lax.axis_index("tensor") // CORES
    rows, cols = keep.shape
    rank, out_block = up.shape
    pieces = [part[:, i * cols : (i + 1) * cols] for i in range(width)]

    def piece(index):
        out = pieces[0]
        for i in range(1, width):
            out = jnp.where(index == i, pieces[i], out)
        return out

    keep[...] = piece(x)
    for shift in range(1, width):
        send = sends[shift - 1]
        send[:rows, :] = piece((x + shift) % width).astype(BF16)
        for i in range(out_block // cols):
            send[pl.ds(rows + i * rank, rank), :] = up[:, i * cols : (i + 1) * cols]


def pick_kernel(sizes, adapter_row, slot_rows, adapters, lengths, slots, bank, after, *rest):
    owners, req_dev, per_owner = sizes
    picks, (table, sem, int_sem) = rest[:owners], rest[owners : owners + 3]
    ints = [
        pltpu.make_async_copy(a, b, int_sem.at[i])
        for i, (a, b) in enumerate(zip((adapters, lengths, slots), rest[owners + 3 :]))
    ]
    for copy in ints:
        copy.start()
    adapters, lengths, slots = rest[owners + 3 :]
    me = lax.axis_index("dp")
    local_slot = slot_rows[...] - me * per_owner
    owned = (local_slot >= 0) & (local_slot < per_owner)
    adapter = lax.broadcasted_iota(jnp.int32, local_slot.shape, 0) * local_slot.shape[1]
    adapter = adapter + lax.broadcasted_iota(jnp.int32, local_slot.shape, 1)
    adapter = jnp.where(owned, adapter, -1)
    local_slot = local_slot.astype(F32)
    served = []
    for home in range(owners):
        value = jnp.zeros(local_slot.shape, F32)
        for q in range(home * req_dev, (home + 1) * req_dev):
            value = jnp.where(adapter == adapter_row[0:1, q : q + 1], local_slot, value)
        served.append(jnp.sum(value).astype(jnp.int32))
    copies = []
    for shift in range(owners):
        index = served[0]
        for home in range(1, owners):
            index = jnp.where((me ^ shift) == home, served[home], index)
        copy = pltpu.make_async_copy(bank.at[index], picks[shift], sem.at[shift])
        copy.start()
        copies.append(copy)
    for copy in ints:
        copy.wait()
    start = jnp.int32(0)
    at = lax.broadcasted_iota(jnp.int32, table.shape, 0)
    lane = lax.broadcasted_iota(jnp.int32, table.shape, 1)
    bounds = jnp.zeros(table.shape, jnp.int32)
    for q in range(req_dev):
        shift = (slots[adapters[me * req_dev + q]] // per_owner) ^ me
        end = start + lengths[me * req_dev + q]
        bounds = jnp.where(at == shift, jnp.where(lane == 0, start, end), bounds)
        start = end
    table[...] = bounds
    for copy in copies:
        copy.wait()


def pack_kernel(order, *refs):
    out = refs[-1]
    for i, s in enumerate(order):
        out[s] = refs[i][...]


def sum_kernel(keep, *rest):
    gots, (out, send) = rest[:-2], rest[-2:]
    total = keep[...]
    for got in gots:
        total = total + got[: total.shape[0], :].astype(F32)
    out[...] = total
    send[...] = total.astype(BF16)


def block_product(width, shift, other, tokens, weight):
    me = lax.axis_index("tensor")
    x, core = me // CORES, me % CORES
    out_block = weight.shape[1] // (width * CORES)
    block = ((x + shift) % width) * CORES + (core + other) % CORES
    columns = pl.ds(pl.multiple_of(block * out_block, out_block), out_block)
    return jnp.dot(tokens[...], weight[:, columns], preferred_element_type=F32)


def far_base_kernel(width, tokens, weight, after, keep, *sends):
    size = sends[0].shape[1]
    for shift in range(1, width):
        other = block_product(width, shift, 1, tokens, weight).astype(BF16)
        for i, send in enumerate(sends):
            send[shift - 1] = other[i * size : (i + 1) * size]
        keep[shift - 1] = block_product(width, shift, 0, tokens, weight)


def mask_kernel(table, after, mask):
    rows, cols = after.shape
    row = lax.broadcasted_iota(jnp.int32, (rows, cols), 0)
    for s in range(mask.shape[1] // cols):
        inside = (row >= table[s : s + 1, 0:1]) & (row < table[s : s + 1, 1:2])
        mask[:, s * cols : (s + 1) * cols] = jnp.where(inside, 1.0, 0.0).astype(BF16)


def near_send_kernel(width, tokens, weight, after, *sends):
    other = block_product(width, 0, 1, tokens, weight).astype(BF16)
    size = sends[0].shape[0]
    for i, send in enumerate(sends):
        send[...] = other[i * size : (i + 1) * size]


def near_keep_kernel(width, tokens, weight, after, keep):
    keep[...] = block_product(width, 0, 0, tokens, weight)


def far_kernel(width, halves, mask, hidden, got_hidden, mine, others, *rest):
    ups, keep, rest = rest[: width - 1], rest[width - 1], rest[width:]
    gots, rest = rest[: -halves * (width - 1) - 3], rest[-halves * (width - 1) - 2 :]
    outs, core_out, rhs = rest[:-2], rest[-2], rest[-1]
    core = lax.axis_index("tensor") % CORES
    owners = mask.shape[1] // hidden.shape[1]
    rank = core_out.shape[1]
    block = hidden.shape[1] // CORES
    owners = mask.shape[1] // hidden.shape[1]
    for s in range(owners):
        for cores, at in ((mine, core), (others, 1 - core)):
            rhs[pl.ds(pl.multiple_of((s * CORES + at) * block, block), block), :] = cores[s]
    total = (hidden[...] + got_hidden[...].astype(F32)).astype(BF16)
    lhs = jnp.concatenate([total] * owners, axis=1) * mask[...]
    part = jnp.dot(lhs, rhs[...], preferred_element_type=F32).astype(BF16)
    core_out[...] = part
    rows = part.shape[0]
    size = rows // halves
    for i in range(width - 1):
        up = jnp.concatenate(
            [ups[i][pl.ds(at, rank), :] for at in range(rows, ups[i].shape[0], rank)], axis=1
        )
        lifted = jnp.dot(part, up, preferred_element_type=F32)
        got = jnp.concatenate([a[i] for a in gots], axis=0).astype(F32)
        sent = (keep[i] + got + lifted).astype(BF16)
        for j in range(halves):
            outs[i * halves + j][...] = sent[j * size : (j + 1) * size]


def near_kernel(up, keep, part, *rest):
    gots, out = rest[:-1], rest[-1]
    lifted = jnp.dot(part[...], up[...], preferred_element_type=F32)
    got = jnp.concatenate([a[...] for a in gots], axis=0).astype(F32)
    out[...] = keep[...] + got + lifted


def final_kernel(halves, near, *rest):
    gots, out = rest[:-1], rest[-1]
    size = near.shape[0] // halves
    for i in range(halves):
        rows = pl.ds(i * size, size)
        total = near[rows, :]
        for got in gots[i::halves]:
            total = total + got[...].astype(F32)
        out[rows, :] = total.astype(BF16)


def local(
    tokens, base_weight, down_basis, up_basis, core_bank, request_adapter, request_length, core_slot
):
    rows, depth = tokens.shape
    out_cols, rank = base_weight.shape[1], down_basis.shape[1]
    owners, tensor = lax.axis_size("dp"), lax.axis_size("tensor")
    width = tensor // CORES
    out_block, block = out_cols // tensor, rank // tensor
    cols = CORES * block
    per_owner = core_bank.shape[0]
    req_dev = request_length.shape[0] // owners
    def pair(a):
        return lax.ppermute(a, "tensor", [(i, i ^ 1) for i in range(tensor)])

    def along_x(a, shift):
        return lax.ppermute(
            a, "tensor", [(i, (i + shift * CORES) % tensor) for i in range(tensor)]
        )

    def along_dp(a, shift):
        return lax.ppermute(a, "dp", [(i, i ^ shift) for i in range(owners)])

    part = jnp.dot(tokens, down_basis, preferred_element_type=F32)
    outs = pl.pallas_call(
        functools.partial(split_kernel, width),
        out_shape=[jax.ShapeDtypeStruct((rows + rank * out_block // cols, cols), BF16)] * (width - 1)
        + [jax.ShapeDtypeStruct((rows, cols), F32)],
        in_specs=[VMEM] * 2,
        out_specs=[VMEM] * width,
        compiler_params=params(),
        cost_estimate=cost(0, 0),
        name="split",
    )(part, up_basis)
    keep = outs[-1]
    gots = [along_x(outs[s - 1], s) for s in range(1, width)]

    outs = pl.pallas_call(
        functools.partial(pick_kernel, (owners, req_dev, per_owner)),
        out_shape=[jax.ShapeDtypeStruct((block, rank), BF16)] * owners
        + [jax.ShapeDtypeStruct((max(owners, 8), 128), jnp.int32)],
        in_specs=[VMEM] * 2 + [ANY] * 5,
        out_specs=[VMEM] * (owners + 1),
        scratch_shapes=[
            pltpu.SemaphoreType.DMA((owners,)),
            pltpu.SemaphoreType.DMA((3,)),
            pltpu.SMEM(request_adapter.shape, jnp.int32),
            pltpu.SMEM(request_length.shape, jnp.int32),
            pltpu.SMEM(core_slot.shape, jnp.int32),
        ],
        compiler_params=params(38),
        cost_estimate=cost(0, 2 * MIB),
        name="pick",
    )(
        request_adapter.reshape(1, -1),
        core_slot.reshape(-1, 128),
        request_adapter,
        request_length,
        core_slot,
        core_bank,
        keep,
    )
    table = outs[-1]
    picks = ordered(outs[:-1], read=30 * MIB)
    order = sorted(range(1, owners), key=lambda s: -s.bit_length())
    mine = [picks[0]] + [along_dp(picks[s], s) for s in order]

    hidden, hidden_send = pl.pallas_call(
        sum_kernel,
        out_shape=[jax.ShapeDtypeStruct((rows, cols), dtype) for dtype in (F32, BF16)],
        in_specs=[VMEM] * width,
        out_specs=[VMEM] * 2,
        compiler_params=params(),
        cost_estimate=cost(0, rows * cols * 10),
        name="hidden_sum",
    )(keep, *gots)
    got_hidden = pair(hidden_send)

    def base(kernel, shapes, after, name, blocks):
        return pl.pallas_call(
            kernel,
            out_shape=shapes,
            in_specs=[VMEM] * (1 + len(after)) + [ANY],
            out_specs=[VMEM] * len(shapes),
            compiler_params=params(),
            cost_estimate=cost(
                2 * rows * depth * out_block * blocks, 2 * depth * (rows + out_block * blocks)
            ),
            name=name,
        )(tokens, base_weight, *after)

    parts = 2
    far_keep, *far_send = base(
        functools.partial(far_base_kernel, width),
        [jax.ShapeDtypeStruct((width - 1, rows, out_block), F32)]
        + [jax.ShapeDtypeStruct((width - 1, rows // parts, out_block), BF16)] * parts,
        [picks[0]],
        "far_base",
        CORES * (width - 1),
    )
    mask = pl.pallas_call(
        mask_kernel,
        out_shape=jax.ShapeDtypeStruct((rows, owners * cols), BF16),
        in_specs=[VMEM, ANY],
        out_specs=VMEM,
        compiler_params=params(),
        cost_estimate=cost(0, 2 * rows * owners * cols),
        name="mask",
    )(table, ordered([hidden], far_keep, down_basis)[0])

    packed = pl.pallas_call(
        functools.partial(pack_kernel, [0] + order),
        out_shape=jax.ShapeDtypeStruct((owners, block, rank), BF16),
        in_specs=[VMEM] * owners + [ANY],
        out_specs=VMEM,
        compiler_params=params(),
        cost_estimate=cost(0, 0),
        name="pack",
    )(*mine, mask)
    got_packed = pair(packed)
    near_send = base(
        functools.partial(near_send_kernel, width),
        [jax.ShapeDtypeStruct((rows // parts, out_block), BF16)] * parts,
        [packed],
        "near_send",
        1,
    )
    far_got = [pair(a) for a in far_send]

    halves = 1
    size = rows // halves
    outs = pl.pallas_call(
        functools.partial(far_kernel, width, halves),
        out_shape=[jax.ShapeDtypeStruct((size, out_block), BF16)] * (halves * (width - 1))
        + [jax.ShapeDtypeStruct((rows, rank), BF16)],
        in_specs=[VMEM] * (5 + width + parts) + [ANY],
        out_specs=[VMEM] * (halves * (width - 1) + 1),
        scratch_shapes=[pltpu.VMEM((owners * cols, rank), BF16)],
        compiler_params=params(),
        cost_estimate=cost(2 * rows * (owners * cols * rank + rank * out_block), rows * out_block * 10),
        name="far",
    )(mask, hidden, got_hidden, packed, got_packed, *gots[::-1], far_keep, *far_got, near_send[0])
    core_out = outs[-1]
    far_gots = [along_x(outs[i], i // halves + 1) for i in range(halves * (width - 1))]

    near_got = [pair(a) for a in ordered(near_send, core_out)]
    (near_keep,) = base(
        functools.partial(near_keep_kernel, width),
        [jax.ShapeDtypeStruct((rows, out_block), F32)],
        [core_out],
        "near_keep",
        1,
    )
    near = pl.pallas_call(
        near_kernel,
        out_shape=jax.ShapeDtypeStruct((rows, out_block), F32),
        in_specs=[VMEM] * (3 + parts),
        out_specs=VMEM,
        compiler_params=params(),
        cost_estimate=cost(2 * rows * rank * out_block, rows * out_block * 12),
        name="near",
    )(up_basis, near_keep, core_out, *near_got)

    return pl.pallas_call(
        functools.partial(final_kernel, halves),
        out_shape=jax.ShapeDtypeStruct((rows, out_block), BF16),
        in_specs=[VMEM] * (1 + len(far_gots)),
        out_specs=VMEM,
        compiler_params=params(),
        cost_estimate=cost(0, rows * out_block * 8),
        name="final",
    )(near, *far_gots)


def solution(mesh):
    in_specs = (
        P(("group", "dp"), "tensor"),
        P("tensor", None),
        P("tensor", None),
        P(None, "tensor"),
        P("dp", "tensor", None),
        P("group"),
        P("group"),
        P("group"),
    )
    out_specs = P(("group", "dp"), "tensor")
    return jax.shard_map(local, mesh=mesh, in_specs=in_specs, out_specs=out_specs, check_vma=False)
```

```python
import functools

import jax
import jax.numpy as jnp
from jax import lax
from jax.experimental import pallas as pl
from jax.experimental.pallas import tpu as pltpu
from jax.sharding import PartitionSpec as P

F32 = jnp.float32
BF16 = jnp.bfloat16
CORES = 2
MIB = 1024 * 1024

ANY = pl.BlockSpec(memory_space=pl.ANY)
VMEM = pl.BlockSpec(memory_space=pltpu.VMEM)


def params(mib=8):
    return pltpu.CompilerParams(vmem_limit_bytes=mib * MIB)


def cost(flops, read):
    return pl.CostEstimate(flops=flops, bytes_accessed=read, transcendentals=0)


def ordered(arrays, *after, read=0):
    count = len(arrays)
    return pl.pallas_call(
        lambda *refs: None,
        out_shape=[jax.ShapeDtypeStruct(a.shape, a.dtype) for a in arrays],
        in_specs=[ANY] * (count + len(after)),
        out_specs=[ANY] * count,
        input_output_aliases={i: i for i in range(count)},
        compiler_params=params(1),
        cost_estimate=cost(0, read),
        name="ordered",
    )(*arrays, *after)


def split_kernel(width, part, up, *rest):
    sends, keep = rest[:-1], rest[-1]
    x = lax.axis_index("tensor") // CORES
    rows, cols = keep.shape
    rank, out_block = up.shape
    pieces = [part[:, i * cols : (i + 1) * cols] for i in range(width)]

    def piece(index):
        out = pieces[0]
        for i in range(1, width):
            out = jnp.where(index == i, pieces[i], out)
        return out

    keep[...] = piece(x)
    for shift in range(1, width):
        send = sends[shift - 1]
        send[:rows, :] = piece((x + shift) % width).astype(BF16)
        for i in range(out_block // cols):
            send[pl.ds(rows + i * rank, rank), :] = up[:, i * cols : (i + 1) * cols]


def pick_kernel(sizes, adapter_row, slot_rows, adapters, lengths, slots, bank, after, *rest):
    owners, req_dev, per_owner = sizes
    picks, (table, sem, int_sem) = rest[:owners], rest[owners : owners + 3]
    ints = [
        pltpu.make_async_copy(a, b, int_sem.at[i])
        for i, (a, b) in enumerate(zip((adapters, lengths, slots), rest[owners + 3 :]))
    ]
    for copy in ints:
        copy.start()
    adapters, lengths, slots = rest[owners + 3 :]
    me = lax.axis_index("dp")
    local_slot = slot_rows[...] - me * per_owner
    owned = (local_slot >= 0) & (local_slot < per_owner)
    adapter = lax.broadcasted_iota(jnp.int32, local_slot.shape, 0) * local_slot.shape[1]
    adapter = adapter + lax.broadcasted_iota(jnp.int32, local_slot.shape, 1)
    adapter = jnp.where(owned, adapter, -1)
    local_slot = local_slot.astype(F32)
    served = []
    for home in range(owners):
        value = jnp.zeros(local_slot.shape, F32)
        for q in range(home * req_dev, (home + 1) * req_dev):
            value = jnp.where(adapter == adapter_row[0:1, q : q + 1], local_slot, value)
        served.append(jnp.sum(value).astype(jnp.int32))
    copies = []
    for shift in range(owners):
        index = served[0]
        for home in range(1, owners):
            index = jnp.where((me ^ shift) == home, served[home], index)
        copy = pltpu.make_async_copy(bank.at[index], picks[shift], sem.at[shift])
        copy.start()
        copies.append(copy)
    for copy in ints:
        copy.wait()
    start = jnp.int32(0)
    at = lax.broadcasted_iota(jnp.int32, table.shape, 0)
    lane = lax.broadcasted_iota(jnp.int32, table.shape, 1)
    bounds = jnp.zeros(table.shape, jnp.int32)
    for q in range(req_dev):
        shift = (slots[adapters[me * req_dev + q]] // per_owner) ^ me
        end = start + lengths[me * req_dev + q]
        bounds = jnp.where(at == shift, jnp.where(lane == 0, start, end), bounds)
        start = end
    table[...] = bounds
    for copy in copies:
        copy.wait()


def pack_kernel(order, *refs):
    out = refs[-1]
    for i, s in enumerate(order):
        out[s] = refs[i][...]


def sum_kernel(keep, *rest):
    gots, (out, send) = rest[:-2], rest[-2:]
    total = keep[...]
    for got in gots:
        total = total + got[: total.shape[0], :].astype(F32)
    out[...] = total
    send[...] = total.astype(BF16)


def block_product(width, shift, other, tokens, weight):
    me = lax.axis_index("tensor")
    x, core = me // CORES, me % CORES
    out_block = weight.shape[1] // (width * CORES)
    block = ((x + shift) % width) * CORES + (core + other) % CORES
    columns = pl.ds(pl.multiple_of(block * out_block, out_block), out_block)
    return jnp.dot(tokens[...], weight[:, columns], preferred_element_type=F32)


def far_base_kernel(width, tokens, weight, after, keep, *sends):
    size = sends[0].shape[1]
    for shift in range(1, width):
        other = block_product(width, shift, 1, tokens, weight).astype(BF16)
        for i, send in enumerate(sends):
            send[shift - 1] = other[i * size : (i + 1) * size]
        keep[shift - 1] = block_product(width, shift, 0, tokens, weight)


def mask_kernel(table, after, mask):
    rows, cols = after.shape
    row = lax.broadcasted_iota(jnp.int32, (rows, cols), 0)
    for s in range(mask.shape[1] // cols):
        inside = (row >= table[s : s + 1, 0:1]) & (row < table[s : s + 1, 1:2])
        mask[:, s * cols : (s + 1) * cols] = jnp.where(inside, 1.0, 0.0).astype(BF16)


def near_send_kernel(width, tokens, weight, after, *sends):
    other = block_product(width, 0, 1, tokens, weight).astype(BF16)
    size = sends[0].shape[0]
    for i, send in enumerate(sends):
        send[...] = other[i * size : (i + 1) * size]


def near_keep_kernel(width, tokens, weight, after, keep):
    keep[...] = block_product(width, 0, 0, tokens, weight)


def far_kernel(width, halves, mask, hidden, got_hidden, mine, others, *rest):
    ups, keep, rest = rest[: width - 1], rest[width - 1], rest[width:]
    gots, rest = rest[: -halves * (width - 1) - 3], rest[-halves * (width - 1) - 2 :]
    outs, core_out, rhs = rest[:-2], rest[-2], rest[-1]
    core = lax.axis_index("tensor") % CORES
    owners = mask.shape[1] // hidden.shape[1]
    rank = core_out.shape[1]
    block = hidden.shape[1] // CORES
    owners = mask.shape[1] // hidden.shape[1]
    for s in range(owners):
        for cores, at in ((mine, core), (others, 1 - core)):
            rhs[pl.ds(pl.multiple_of((s * CORES + at) * block, block), block), :] = cores[s]
    total = (hidden[...] + got_hidden[...].astype(F32)).astype(BF16)
    lhs = jnp.concatenate([total] * owners, axis=1) * mask[...]
    part = jnp.dot(lhs, rhs[...], preferred_element_type=F32).astype(BF16)
    core_out[...] = part
    rows = part.shape[0]
    size = rows // halves
    for i in range(width - 1):
        up = jnp.concatenate(
            [ups[i][pl.ds(at, rank), :] for at in range(rows, ups[i].shape[0], rank)], axis=1
        )
        lifted = jnp.dot(part, up, preferred_element_type=F32)
        got = jnp.concatenate([a[i] for a in gots], axis=0).astype(F32)
        sent = (keep[i] + got + lifted).astype(BF16)
        for j in range(halves):
            outs[i * halves + j][...] = sent[j * size : (j + 1) * size]


def near_kernel(up, keep, part, *rest):
    gots, out = rest[:-1], rest[-1]
    lifted = jnp.dot(part[...], up[...], preferred_element_type=F32)
    got = jnp.concatenate([a[...] for a in gots], axis=0).astype(F32)
    out[...] = keep[...] + got + lifted


def final_kernel(halves, near, *rest):
    gots, (out, buf, sem) = rest[:-3], rest[-3:]
    rows = near.shape[0]
    size = rows // 2
    copies = []
    for i in range(2):
        at = slice(i * size, (i + 1) * size)
        total = near[at, :]
        for got in gots:
            total = total + got[at, :].astype(F32)
        buf[at, :] = total.astype(BF16)
        copies.append(
            pltpu.make_async_copy(
                buf.at[pl.ds(i * size, size)], out.at[pl.ds(i * size, size)], sem.at[i]
            )
        )
        copies[-1].start()
    for copy in copies:
        copy.wait()


def local(
    tokens, base_weight, down_basis, up_basis, core_bank, request_adapter, request_length, core_slot
):
    rows, depth = tokens.shape
    out_cols, rank = base_weight.shape[1], down_basis.shape[1]
    owners, tensor = lax.axis_size("dp"), lax.axis_size("tensor")
    width = tensor // CORES
    out_block, block = out_cols // tensor, rank // tensor
    cols = CORES * block
    per_owner = core_bank.shape[0]
    req_dev = request_length.shape[0] // owners
    def pair(a):
        return lax.ppermute(a, "tensor", [(i, i ^ 1) for i in range(tensor)])

    def along_x(a, shift):
        return lax.ppermute(
            a, "tensor", [(i, (i + shift * CORES) % tensor) for i in range(tensor)]
        )

    def along_dp(a, shift):
        return lax.ppermute(a, "dp", [(i, i ^ shift) for i in range(owners)])

    part = jnp.dot(tokens, down_basis, preferred_element_type=F32)
    outs = pl.pallas_call(
        functools.partial(split_kernel, width),
        out_shape=[jax.ShapeDtypeStruct((rows + rank * out_block // cols, cols), BF16)] * (width - 1)
        + [jax.ShapeDtypeStruct((rows, cols), F32)],
        in_specs=[VMEM] * 2,
        out_specs=[VMEM] * width,
        compiler_params=params(),
        cost_estimate=cost(0, 0),
        name="split",
    )(part, up_basis)
    keep = outs[-1]
    gots = [along_x(outs[s - 1], s) for s in range(1, width)]

    outs = pl.pallas_call(
        functools.partial(pick_kernel, (owners, req_dev, per_owner)),
        out_shape=[jax.ShapeDtypeStruct((block, rank), BF16)] * owners
        + [jax.ShapeDtypeStruct((max(owners, 8), 128), jnp.int32)],
        in_specs=[VMEM] * 2 + [ANY] * 5,
        out_specs=[VMEM] * (owners + 1),
        scratch_shapes=[
            pltpu.SemaphoreType.DMA((owners,)),
            pltpu.SemaphoreType.DMA((3,)),
            pltpu.SMEM(request_adapter.shape, jnp.int32),
            pltpu.SMEM(request_length.shape, jnp.int32),
            pltpu.SMEM(core_slot.shape, jnp.int32),
        ],
        compiler_params=params(38),
        cost_estimate=cost(0, 2 * MIB),
        name="pick",
    )(
        request_adapter.reshape(1, -1),
        core_slot.reshape(-1, 128),
        request_adapter,
        request_length,
        core_slot,
        core_bank,
        keep,
    )
    table = outs[-1]
    picks = ordered(outs[:-1], read=30 * MIB)
    order = sorted(range(1, owners), key=lambda s: -s.bit_length())
    mine = [picks[0]] + [along_dp(picks[s], s) for s in order]

    hidden, hidden_send = pl.pallas_call(
        sum_kernel,
        out_shape=[jax.ShapeDtypeStruct((rows, cols), dtype) for dtype in (F32, BF16)],
        in_specs=[VMEM] * width,
        out_specs=[VMEM] * 2,
        compiler_params=params(),
        cost_estimate=cost(0, rows * cols * 10),
        name="hidden_sum",
    )(keep, *gots)
    got_hidden = pair(hidden_send)

    def base(kernel, shapes, after, name, blocks):
        return pl.pallas_call(
            kernel,
            out_shape=shapes,
            in_specs=[VMEM] * (1 + len(after)) + [ANY],
            out_specs=[VMEM] * len(shapes),
            compiler_params=params(),
            cost_estimate=cost(
                2 * rows * depth * out_block * blocks, 2 * depth * (rows + out_block * blocks)
            ),
            name=name,
        )(tokens, base_weight, *after)

    parts = 2
    far_keep, *far_send = base(
        functools.partial(far_base_kernel, width),
        [jax.ShapeDtypeStruct((width - 1, rows, out_block), F32)]
        + [jax.ShapeDtypeStruct((width - 1, rows // parts, out_block), BF16)] * parts,
        [picks[0]],
        "far_base",
        CORES * (width - 1),
    )
    mask = pl.pallas_call(
        mask_kernel,
        out_shape=jax.ShapeDtypeStruct((rows, owners * cols), BF16),
        in_specs=[VMEM, ANY],
        out_specs=VMEM,
        compiler_params=params(),
        cost_estimate=cost(0, 2 * rows * owners * cols),
        name="mask",
    )(table, ordered([hidden], far_keep, down_basis)[0])

    packed = pl.pallas_call(
        functools.partial(pack_kernel, [0] + order),
        out_shape=jax.ShapeDtypeStruct((owners, block, rank), BF16),
        in_specs=[VMEM] * owners + [ANY],
        out_specs=VMEM,
        compiler_params=params(),
        cost_estimate=cost(0, 0),
        name="pack",
    )(*mine, mask)
    got_packed = pair(packed)
    near_send = base(
        functools.partial(near_send_kernel, width),
        [jax.ShapeDtypeStruct((rows // parts, out_block), BF16)] * parts,
        [packed],
        "near_send",
        1,
    )
    far_got = [pair(a) for a in far_send]

    halves = 1
    size = rows // halves
    outs = pl.pallas_call(
        functools.partial(far_kernel, width, halves),
        out_shape=[jax.ShapeDtypeStruct((size, out_block), BF16)] * (halves * (width - 1))
        + [jax.ShapeDtypeStruct((rows, rank), BF16)],
        in_specs=[VMEM] * (5 + width + parts) + [ANY],
        out_specs=[VMEM] * (halves * (width - 1) + 1),
        scratch_shapes=[pltpu.VMEM((owners * cols, rank), BF16)],
        compiler_params=params(),
        cost_estimate=cost(2 * rows * (owners * cols * rank + rank * out_block), rows * out_block * 10),
        name="far",
    )(mask, hidden, got_hidden, packed, got_packed, *gots[::-1], far_keep, *far_got, near_send[0])
    core_out = outs[-1]
    far_gots = [along_x(outs[i], i // halves + 1) for i in range(halves * (width - 1))]

    near_got = [pair(a) for a in ordered(near_send, core_out)]
    (near_keep,) = base(
        functools.partial(near_keep_kernel, width),
        [jax.ShapeDtypeStruct((rows, out_block), F32)],
        [core_out],
        "near_keep",
        1,
    )
    near = pl.pallas_call(
        near_kernel,
        out_shape=jax.ShapeDtypeStruct((rows, out_block), F32),
        in_specs=[VMEM] * (3 + parts),
        out_specs=VMEM,
        compiler_params=params(),
        cost_estimate=cost(2 * rows * rank * out_block, rows * out_block * 12),
        name="near",
    )(up_basis, near_keep, core_out, *near_got)

    return pl.pallas_call(
        functools.partial(final_kernel, halves),
        out_shape=jax.ShapeDtypeStruct((rows, out_block), BF16),
        in_specs=[VMEM] * (1 + len(far_gots)),
        out_specs=ANY,
        scratch_shapes=[pltpu.VMEM((rows, out_block), BF16), pltpu.SemaphoreType.DMA((2,))],
        compiler_params=params(),
        cost_estimate=cost(0, rows * out_block * 8),
        name="final",
    )(near, *far_gots)


def solution(mesh):
    in_specs = (
        P(("group", "dp"), "tensor"),
        P("tensor", None),
        P("tensor", None),
        P(None, "tensor"),
        P("dp", "tensor", None),
        P("group"),
        P("group"),
        P("group"),
    )
    out_specs = P(("group", "dp"), "tensor")
    return jax.shard_map(local, mesh=mesh, in_specs=in_specs, out_specs=out_specs, check_vma=False)
```

```python
import functools

import jax
import jax.numpy as jnp
from jax import lax
from jax.experimental import pallas as pl
from jax.experimental.pallas import tpu as pltpu
from jax.sharding import PartitionSpec as P

F32 = jnp.float32
BF16 = jnp.bfloat16
CORES = 2
MIB = 1024 * 1024

ANY = pl.BlockSpec(memory_space=pl.ANY)
VMEM = pl.BlockSpec(memory_space=pltpu.VMEM)


def params(mib=8):
    return pltpu.CompilerParams(vmem_limit_bytes=mib * MIB)


def cost(flops, read):
    return pl.CostEstimate(flops=flops, bytes_accessed=read, transcendentals=0)


def ordered(arrays, *after, read=0):
    count = len(arrays)
    return pl.pallas_call(
        lambda *refs: None,
        out_shape=[jax.ShapeDtypeStruct(a.shape, a.dtype) for a in arrays],
        in_specs=[ANY] * (count + len(after)),
        out_specs=[ANY] * count,
        input_output_aliases={i: i for i in range(count)},
        compiler_params=params(1),
        cost_estimate=cost(0, read),
        name="ordered",
    )(*arrays, *after)


def split_kernel(width, part, up, *rest):
    sends, keep = rest[:-1], rest[-1]
    x = lax.axis_index("tensor") // CORES
    rows, cols = keep.shape
    rank, out_block = up.shape
    pieces = [part[:, i * cols : (i + 1) * cols] for i in range(width)]

    def piece(index):
        out = pieces[0]
        for i in range(1, width):
            out = jnp.where(index == i, pieces[i], out)
        return out

    keep[...] = piece(x)
    for shift in range(1, width):
        send = sends[shift - 1]
        send[:rows, :] = piece((x + shift) % width).astype(BF16)
        for i in range(out_block // cols):
            send[pl.ds(rows + i * rank, rank), :] = up[:, i * cols : (i + 1) * cols]


def pick_kernel(sizes, adapter_row, slot_rows, adapters, lengths, slots, bank, after, *rest):
    owners, req_dev, per_owner = sizes
    picks, (table, sem, int_sem) = rest[:owners], rest[owners : owners + 3]
    ints = [
        pltpu.make_async_copy(a, b, int_sem.at[i])
        for i, (a, b) in enumerate(zip((adapters, lengths, slots), rest[owners + 3 :]))
    ]
    for copy in ints:
        copy.start()
    adapters, lengths, slots = rest[owners + 3 :]
    me = lax.axis_index("dp")
    local_slot = slot_rows[...] - me * per_owner
    owned = (local_slot >= 0) & (local_slot < per_owner)
    adapter = lax.broadcasted_iota(jnp.int32, local_slot.shape, 0) * local_slot.shape[1]
    adapter = adapter + lax.broadcasted_iota(jnp.int32, local_slot.shape, 1)
    adapter = jnp.where(owned, adapter, -1)
    local_slot = local_slot.astype(F32)
    served = []
    for home in range(owners):
        value = jnp.zeros(local_slot.shape, F32)
        for q in range(home * req_dev, (home + 1) * req_dev):
            value = jnp.where(adapter == adapter_row[0:1, q : q + 1], local_slot, value)
        served.append(jnp.sum(value).astype(jnp.int32))
    copies = []
    for shift in range(owners):
        index = served[0]
        for home in range(1, owners):
            index = jnp.where((me ^ shift) == home, served[home], index)
        copy = pltpu.make_async_copy(bank.at[index], picks[shift], sem.at[shift])
        copy.start()
        copies.append(copy)
    for copy in ints:
        copy.wait()
    start = jnp.int32(0)
    at = lax.broadcasted_iota(jnp.int32, table.shape, 0)
    lane = lax.broadcasted_iota(jnp.int32, table.shape, 1)
    bounds = jnp.zeros(table.shape, jnp.int32)
    for q in range(req_dev):
        shift = (slots[adapters[me * req_dev + q]] // per_owner) ^ me
        end = start + lengths[me * req_dev + q]
        bounds = jnp.where(at == shift, jnp.where(lane == 0, start, end), bounds)
        start = end
    table[...] = bounds
    for copy in copies:
        copy.wait()


def pack_kernel(order, *refs):
    out = refs[-1]
    for i, s in enumerate(order):
        out[s] = refs[i][...]


def sum_kernel(keep, *rest):
    gots, (out, send) = rest[:-2], rest[-2:]
    total = keep[...]
    for got in gots:
        total = total + got[: total.shape[0], :].astype(F32)
    out[...] = total
    send[...] = total.astype(BF16)


def block_product(width, shift, other, tokens, weight):
    me = lax.axis_index("tensor")
    x, core = me // CORES, me % CORES
    out_block = weight.shape[1] // (width * CORES)
    block = ((x + shift) % width) * CORES + (core + other) % CORES
    columns = pl.ds(pl.multiple_of(block * out_block, out_block), out_block)
    return jnp.dot(tokens[...], weight[:, columns], preferred_element_type=F32)


def far_base_kernel(width, tokens, weight, after, keep, *sends):
    size = sends[0].shape[1]
    for shift in range(1, width):
        other = block_product(width, shift, 1, tokens, weight).astype(BF16)
        for i, send in enumerate(sends):
            send[shift - 1] = other[i * size : (i + 1) * size]
        keep[shift - 1] = block_product(width, shift, 0, tokens, weight)


def mask_kernel(table, after, mask):
    rows, cols = after.shape
    row = lax.broadcasted_iota(jnp.int32, (rows, cols), 0)
    for s in range(mask.shape[1] // cols):
        inside = (row >= table[s : s + 1, 0:1]) & (row < table[s : s + 1, 1:2])
        mask[:, s * cols : (s + 1) * cols] = jnp.where(inside, 1.0, 0.0).astype(BF16)


def near_send_kernel(width, tokens, weight, after, *sends):
    other = block_product(width, 0, 1, tokens, weight).astype(BF16)
    size = sends[0].shape[0]
    for i, send in enumerate(sends):
        send[...] = other[i * size : (i + 1) * size]


def near_keep_kernel(width, tokens, weight, after, keep):
    keep[...] = block_product(width, 0, 0, tokens, weight)


def far_kernel(width, at, mask, hidden, got_hidden, mine, others, *rest):
    ups, keep, rest = rest[: width - 1], rest[width - 1], rest[width:]
    gots, rest = rest[: -width - 2], rest[-width - 1 :]
    outs, core_out, rhs = rest[:-2], rest[-2], rest[-1]
    core = lax.axis_index("tensor") % CORES
    owners = mask.shape[1] // hidden.shape[1]
    size, rank = core_out.shape
    rows, block = hidden.shape[0], hidden.shape[1] // CORES
    for s in range(owners):
        for cores, half in ((mine, core), (others, 1 - core)):
            to = pl.multiple_of((s * CORES + half) * block, block)
            rhs[pl.ds(to, block), :] = cores[s]
    total = (hidden[at : at + size, :] + got_hidden[at : at + size, :].astype(F32)).astype(BF16)
    lhs = jnp.concatenate([total] * owners, axis=1) * mask[at : at + size, :]
    part = jnp.dot(lhs, rhs[...], preferred_element_type=F32).astype(BF16)
    core_out[...] = part
    for i in range(width - 1):
        up = jnp.concatenate(
            [ups[i][pl.ds(r, rank), :] for r in range(rows, ups[i].shape[0], rank)], axis=1
        )
        lifted = jnp.dot(part, up, preferred_element_type=F32)
        got = jnp.concatenate([a[i] for a in gots], axis=0)[at : at + size].astype(F32)
        outs[i][...] = (keep[i, at : at + size, :] + got + lifted).astype(BF16)


def near_kernel(parts, up, keep, *rest):
    core_outs, gots, out = rest[:-parts - 1], rest[-parts - 1 : -1], rest[-1]
    got = jnp.concatenate([a[...] for a in gots], axis=0).astype(F32)
    at = 0
    for part in core_outs:
        to = at + part.shape[0]
        lifted = jnp.dot(part[...], up[...], preferred_element_type=F32)
        out[at:to, :] = keep[at:to, :] + got[at:to] + lifted
        at = to


def final_kernel(pieces, near, *rest):
    gots, out = rest[:-1], rest[-1]
    at = 0
    for i in range(pieces):
        to = at + gots[i].shape[0]
        total = near[at:to, :]
        for got in gots[i::pieces]:
            total = total + got[...].astype(F32)
        out[at:to, :] = total.astype(BF16)
        at = to


def local(
    tokens, base_weight, down_basis, up_basis, core_bank, request_adapter, request_length, core_slot
):
    rows, depth = tokens.shape
    out_cols, rank = base_weight.shape[1], down_basis.shape[1]
    owners, tensor = lax.axis_size("dp"), lax.axis_size("tensor")
    width = tensor // CORES
    out_block, block = out_cols // tensor, rank // tensor
    cols = CORES * block
    per_owner = core_bank.shape[0]
    req_dev = request_length.shape[0] // owners
    def pair(a):
        return lax.ppermute(a, "tensor", [(i, i ^ 1) for i in range(tensor)])

    def along_x(a, shift):
        return lax.ppermute(
            a, "tensor", [(i, (i + shift * CORES) % tensor) for i in range(tensor)]
        )

    def along_dp(a, shift):
        return lax.ppermute(a, "dp", [(i, i ^ shift) for i in range(owners)])

    part = jnp.dot(tokens, down_basis, preferred_element_type=F32)
    outs = pl.pallas_call(
        functools.partial(split_kernel, width),
        out_shape=[jax.ShapeDtypeStruct((rows + rank * out_block // cols, cols), BF16)] * (width - 1)
        + [jax.ShapeDtypeStruct((rows, cols), F32)],
        in_specs=[VMEM] * 2,
        out_specs=[VMEM] * width,
        compiler_params=params(),
        cost_estimate=cost(0, 0),
        name="split",
    )(part, up_basis)
    keep = outs[-1]
    gots = [along_x(outs[s - 1], s) for s in range(1, width)]

    outs = pl.pallas_call(
        functools.partial(pick_kernel, (owners, req_dev, per_owner)),
        out_shape=[jax.ShapeDtypeStruct((block, rank), BF16)] * owners
        + [jax.ShapeDtypeStruct((max(owners, 8), 128), jnp.int32)],
        in_specs=[VMEM] * 2 + [ANY] * 5,
        out_specs=[VMEM] * (owners + 1),
        scratch_shapes=[
            pltpu.SemaphoreType.DMA((owners,)),
            pltpu.SemaphoreType.DMA((3,)),
            pltpu.SMEM(request_adapter.shape, jnp.int32),
            pltpu.SMEM(request_length.shape, jnp.int32),
            pltpu.SMEM(core_slot.shape, jnp.int32),
        ],
        compiler_params=params(38),
        cost_estimate=cost(0, 2 * MIB),
        name="pick",
    )(
        request_adapter.reshape(1, -1),
        core_slot.reshape(-1, 128),
        request_adapter,
        request_length,
        core_slot,
        core_bank,
        keep,
    )
    table = outs[-1]
    picks = ordered(outs[:-1], read=30 * MIB)
    order = sorted(range(1, owners), key=lambda s: -s.bit_length())
    mine = [picks[0]] + [along_dp(picks[s], s) for s in order]

    hidden, hidden_send = pl.pallas_call(
        sum_kernel,
        out_shape=[jax.ShapeDtypeStruct((rows, cols), dtype) for dtype in (F32, BF16)],
        in_specs=[VMEM] * width,
        out_specs=[VMEM] * 2,
        compiler_params=params(),
        cost_estimate=cost(0, rows * cols * 10),
        name="hidden_sum",
    )(keep, *gots)
    got_hidden = pair(hidden_send)

    def base(kernel, shapes, after, name, blocks):
        return pl.pallas_call(
            kernel,
            out_shape=shapes,
            in_specs=[VMEM] * (1 + len(after)) + [ANY],
            out_specs=[VMEM] * len(shapes),
            compiler_params=params(),
            cost_estimate=cost(
                2 * rows * depth * out_block * blocks, 2 * depth * (rows + out_block * blocks)
            ),
            name=name,
        )(tokens, base_weight, *after)

    parts = 2
    far_keep, *far_send = base(
        functools.partial(far_base_kernel, width),
        [jax.ShapeDtypeStruct((width - 1, rows, out_block), F32)]
        + [jax.ShapeDtypeStruct((width - 1, rows // parts, out_block), BF16)] * parts,
        [picks[0]],
        "far_base",
        CORES * (width - 1),
    )
    mask = pl.pallas_call(
        mask_kernel,
        out_shape=jax.ShapeDtypeStruct((rows, owners * cols), BF16),
        in_specs=[VMEM, ANY],
        out_specs=VMEM,
        compiler_params=params(),
        cost_estimate=cost(0, 2 * rows * owners * cols),
        name="mask",
    )(table, ordered([hidden], far_keep, down_basis)[0])

    packed = pl.pallas_call(
        functools.partial(pack_kernel, [0] + order),
        out_shape=jax.ShapeDtypeStruct((owners, block, rank), BF16),
        in_specs=[VMEM] * owners + [ANY],
        out_specs=VMEM,
        compiler_params=params(),
        cost_estimate=cost(0, 0),
        name="pack",
    )(*mine, mask)
    got_packed = pair(packed)
    near_send = base(
        functools.partial(near_send_kernel, width),
        [jax.ShapeDtypeStruct((rows // parts, out_block), BF16)] * parts,
        [packed],
        "near_send",
        1,
    )
    far_got = [pair(a) for a in far_send]

    first = rows * 3 // 5 // 16 * 16
    pieces = [(0, first), (first, rows - first)]
    core_outs, sent = [], []
    for at, size in pieces:
        outs = pl.pallas_call(
            functools.partial(far_kernel, width, at),
            out_shape=[jax.ShapeDtypeStruct((size, out_block), BF16)] * (width - 1)
            + [jax.ShapeDtypeStruct((size, rank), BF16)],
            in_specs=[VMEM] * (5 + width + parts) + [ANY],
            out_specs=[VMEM] * width,
            scratch_shapes=[pltpu.VMEM((owners * cols, rank), BF16)],
            compiler_params=params(),
            cost_estimate=cost(2 * size * (owners * cols * rank + rank * out_block), size * out_block * 10),
            name="far",
        )(
            mask, hidden, got_hidden, packed, got_packed, *gots[::-1], far_keep, *far_got,
            core_outs[-1] if core_outs else near_send[0],
        )
        sent.append([along_x(outs[s - 1], s) for s in range(1, width)])
        core_outs.append(outs[-1])
    far_gots = [piece[s] for s in range(width - 1) for piece in sent]

    near_got = [pair(a) for a in ordered(near_send, core_outs[0])]
    (near_keep,) = base(
        functools.partial(near_keep_kernel, width),
        [jax.ShapeDtypeStruct((rows, out_block), F32)],
        [core_outs[0]],
        "near_keep",
        1,
    )
    near = pl.pallas_call(
        functools.partial(near_kernel, parts),
        out_shape=jax.ShapeDtypeStruct((rows, out_block), F32),
        in_specs=[VMEM] * (2 + len(pieces) + parts),
        out_specs=VMEM,
        compiler_params=params(),
        cost_estimate=cost(2 * rows * rank * out_block, rows * out_block * 12),
        name="near",
    )(up_basis, near_keep, *core_outs, *near_got)

    return pl.pallas_call(
        functools.partial(final_kernel, len(pieces)),
        out_shape=jax.ShapeDtypeStruct((rows, out_block), BF16),
        in_specs=[VMEM] * (1 + len(far_gots)),
        out_specs=VMEM,
        compiler_params=params(),
        cost_estimate=cost(0, rows * out_block * 8),
        name="final",
    )(near, *far_gots)


def solution(mesh):
    in_specs = (
        P(("group", "dp"), "tensor"),
        P("tensor", None),
        P("tensor", None),
        P(None, "tensor"),
        P("dp", "tensor", None),
        P("group"),
        P("group"),
        P("group"),
    )
    out_specs = P(("group", "dp"), "tensor")
    return jax.shard_map(local, mesh=mesh, in_specs=in_specs, out_specs=out_specs, check_vma=False)
```
